128 devices in a mesh: tok: 8 (over x, core), feat: 16 (over z, y).
Axes of the slice: x: 4, y: 4, z: 4, core: 2. Of those that a mesh axis runs over, the one named last changes fastest.
Arguments:
- activations: bfloat16 [8192, 28672], P('tok', 'feat'), may hold values from -6 to 6
- out_grads: bfloat16 [8192, 8192], P('tok', 'feat'), may hold values from -6 to 6
- query_out: bfloat16 [64, 32, 8192], P('tok', None, 'feat'), may hold values from -0.0625 to 0.0625
- query_in: bfloat16 [64, 32, 28672], P('tok', None, 'feat'), may hold values from -0.03125 to 0.03125
Outputs:
- influence: float32 [8192, 64], P(('tok', 'feat'))
The draws below stay inside these ranges and needn't reach their ends.
All inputs are finite; a program needn't handle non-finite values.
Results may differ from the reference program's by a relative error of at most 0.0003.
Values may be sent and summed in bfloat16 or wider, within the bound.
A program may use at most 128 MiB of HBM per device.

```python
import jax
import jax.numpy as jnp
from jax import lax

D = 8192
FF = 28672
RANK = 32
TOKENS = 8192
NQ = 64


def steps_of(key, dims, cuts, least, top_value):
    def one(dim, parts):
        steps = jax.random.uniform(jax.random.fold_in(jax.random.fold_in(key, 6), dim), (parts,), jnp.float32, least / len(cuts), top_value / len(cuts))
        return jnp.repeat(jnp.exp(steps), dims[dim] // parts).reshape((-1,) + (1,) * (len(dims) - dim - 1))

    loudness = one(*cuts[0])
    for cut in cuts[1:]:
        loudness = loudness * one(*cut)
    return loudness


def bell_draw(own_key, dims, width, bound, split=(), kind=jnp.bfloat16):
    array = jax.random.normal(own_key, dims, jnp.float32) * width
    if len(split) > 0:
        array = steps_of(own_key, dims, split, -0.22, 0.18) * array
    return jnp.clip(array, min=-bound, max=bound).astype(kind)


def setup_inputs(seed: int = 0) -> dict:
    splits = jax.random.split(jax.random.key(seed), 5)
    return {
        "activations": bell_draw(splits[0], (TOKENS, FF), 1.0, 6.0, ((0, 8), (1, 16))),
        "out_grads": bell_draw(splits[1], (TOKENS, D), 1.0, 6.0, ((0, 8), (1, 16))),
        "query_out": bell_draw(splits[2], (NQ, RANK, D), D ** -0.5, 0.0625, ((0, 8), (2, 16))),
        "query_in": bell_draw(splits[3], (NQ, RANK, FF), FF ** -0.5, 0.03125, ((0, 8), (2, 16))),
    }


def reference(activations, out_grads, query_out, query_in):
    def one_query(pair):
        outer, inner = pair
        grad_proj = jnp.dot(out_grads, outer.T, preferred_element_type=jnp.float32)
        act_proj = jnp.dot(activations, inner.T, preferred_element_type=jnp.float32)
        return jnp.sum(grad_proj * act_proj, axis=1) * (RANK ** -0.5)

    scores = lax.map(one_query, (query_out, query_in))
    return scores.T
```

```python
import jax
import jax.numpy as jnp
from jax import lax
from jax.experimental import pallas as pl
from jax.experimental.pallas import tpu as pltpu
from jax.sharding import PartitionSpec as P

RANK = 32
MESH = pl.DeviceIdType.MESH
F32 = jnp.float32
BF16 = jnp.bfloat16

STREAMS = 4
LEVELS = 4
STEPS = 8
SLOTS = 5
POWER = 17
TOP = 2.0 ** (127.0 / POWER)
TINY = 2.0**-100
IDLE = (2,)
TURNS = STEPS + len(IDLE) + LEVELS
NEAR_A, NEAR_B, FAR = (2, 5), (3, 6), (4, 7)


def flip_one(v):
    return v + 1 - 2 * (v % 2)


def flip_three(v):
    return 3 - v


def encode(value, inverse):
    n = value * inverse
    n2 = n * n
    n4 = n2 * n2
    n8 = n4 * n4
    return (n8 * n8 * n).astype(BF16)


def decode(sent, scale):
    y = sent.astype(F32)
    log = jnp.log2(jnp.maximum(jnp.abs(y), 2.0**-126))
    return y * jnp.exp2(log * (1.0 / POWER - 1.0)) * scale


def bound_above(bound):
    return jnp.maximum((bound * 1.01).astype(BF16).astype(F32), TINY)


def tiles(value):
    return value.reshape(value.shape[0] // 8, 8, 128)


def rows_of(value):
    return value.reshape(value.shape[0] * 8, 128)


def kernel(
    act, og, qi, qo, out,
    a_v, g_v, qi_v, qo_v, part, bounds, prod,
    s1, s2, s3, s4, r1, r2, r3, r4,
    load_sem, own_sem, q_send, q_recv, m_send, m_recv,
):
    tok = lax.axis_index("tok")
    feat = lax.axis_index("feat")
    x, core = tok // 2, tok % 2
    z, y = feat // 4, feat % 4
    sibling = (tok + 1 - 2 * core, feat)
    near_a = (flip_one(x) * 2 + core, feat)
    near_b = (flip_three(x) * 2 + core, feat)
    partners = (
        (tok, z * 4 + flip_one(y)),
        (tok, z * 4 + flip_three(y)),
        (tok, flip_one(z) * 4 + y),
        (tok, flip_three(z) * 4 + y),
    )
    sends, recvs = (s1, s2, s3, s4), (r1, r2, r3, r4)

    own = []
    for h in range(2):
        for a, (src, dst) in enumerate(((qi, qi_v), (qo, qo_v))):
            copy = pltpu.make_async_copy(src.at[pl.ds(h * 128, 128)], dst.at[h, core], own_sem.at[a, h])
            copy.start()
            own.append(copy)

    def load(n, carry):
        half = 1 - n // 32
        k = (n // 8) % 4
        position = (1 - n // 32) * 8 + n % 8
        bits = [(position // 8) % 2, (position // 4) % 2, (position // 2) % 2, position % 2]
        flips = []
        for d in range(4):
            j = (d - k + 4) % 4
            flips.append((position // (8 // (1 + j % 2 + (j // 2) * 3 + (j // 2) * (j % 2) * 3))) % 2)
        y1 = y + flips[0] * (1 - 2 * (y % 2))
        y2 = y1 + flips[1] * (3 - 2 * y1)
        z1 = z + flips[2] * (1 - 2 * (z % 2))
        z2 = z1 + flips[3] * (3 - 2 * z1)
        row = pl.multiple_of((z2 * 4 + y2) * 64 + k * 16, 16)
        place = pl.multiple_of(half * 512 + k * 128 + (position % 8) * 16, 16)
        pltpu.make_async_copy(og.at[pl.ds(row, 16)], g_v.at[pl.ds(place, 16)], load_sem.at[1]).start()
        pltpu.make_async_copy(act.at[pl.ds(row, 16)], a_v.at[pl.ds(place, 16)], load_sem.at[0]).start()
        return carry

    lax.fori_loop(0, 64, load, 0)

    barrier = pltpu.get_barrier_semaphore()
    for device in (sibling, near_a, near_b) + partners:
        pl.semaphore_signal(barrier, inc=1, device_id=device, device_id_type=MESH)
    pl.semaphore_wait(barrier, 7)

    def query_copy(a, h, j):
        src, dst = ((qi, qi_v), (qo, qo_v))[a]
        to = (sibling, near_a, near_b, sibling, sibling, near_b, near_a, sibling)[j]
        if j < 3:
            source = src.at[pl.ds(h * 128, 128)]
            target = dst.at[(h, NEAR_A[h], NEAR_B[h])[j], core]
        elif j in (3, 4, 7):
            source = target = dst.at[{3: NEAR_A, 4: NEAR_B, 7: FAR}[j][h], core]
        else:
            half = pl.ds((j - 5) * 64, 64)
            source = dst.at[(NEAR_A, NEAR_B)[j - 5][h], core, half]
            target = dst.at[FAR[h], core, half]
        return pltpu.make_async_remote_copy(
            source, target, q_send.at[a, h, j], q_recv.at[a, h, j], device_id=to, device_id_type=MESH
        )

    def start_queries(h, js):
        for j in js:
            for a in range(2):
                query_copy(a, h, j).start()

    def await_queries(h, j):
        for a in range(2):
            query_copy(a, h, j).wait_recv()

    start_queries(0, (0, 1, 2))
    start_queries(1, (0,))

    def message(step, level, k):
        return pltpu.make_async_remote_copy(
            sends[level].at[step, k], recvs[level].at[step, k], m_send.at[step, level, k], m_recv.at[step, level, k],
            device_id=partners[(k + level) % 4], device_id_type=MESH,
        )

    def arrivals(step):
        for h in range(2):
            @pl.when(step == h)
            def _():
                own[2 * h].wait()
                own[2 * h + 1].wait()
                await_queries(h, 0)

            @pl.when(step == NEAR_A[h])
            def _():
                await_queries(h, 1)
                start_queries(h, (5, 3))
                await_queries(h, 2)
                start_queries(h, (6, 4))
                if h == 0:
                    start_queries(1, (1, 2))
                await_queries(h, 3)

            @pl.when(step == NEAR_B[h])
            def _():
                await_queries(h, 4)

            @pl.when(step == FAR[h])
            def _():
                await_queries(h, 5)
                await_queries(h, 6)
                start_queries(h, (7,))
                await_queries(h, 7)

        @pl.when(step == 0)
        def _():
            pltpu.make_async_copy(og, g_v, load_sem.at[1]).wait()
            pltpu.make_async_copy(act, a_v, load_sem.at[0]).wait()

    def multiply(step):
        slot = step % SLOTS
        for t, (tokens, queries) in enumerate(((a_v, qi_v), (g_v, qo_v))):
            weights = queries[step].reshape(256, queries.shape[3])
            for m in range(2):
                block = lax.dot_general(
                    tokens[pl.ds(m * 512, 512), :], weights, (((1,), (1,)), ((), ())), preferred_element_type=F32
                )
                part[slot, 2 * t, pl.ds(m * 512, 512), :] = block[:, :128]
                part[slot, 2 * t + 1, pl.ds(m * 512, 512), :] = block[:, 128:]
        inverse, top_bounds = [], []
        for t in range(2):
            top = jnp.max(jnp.abs(part[slot, pl.ds(2 * t, 2)].reshape(256, 8, 128)), axis=0)
            top = jnp.max(jnp.max(top, axis=1, keepdims=True), axis=0, keepdims=True)
            bound = bound_above(jnp.broadcast_to(top, (8, 128)))
            for k in range(STREAMS):
                bounds[slot, k, t] = bound
            top_bounds.append(bound)
            inverse.append(TOP / bound)
        for k in range(STREAMS):
            s1[step, k, pl.ds(512, 16), :] = jnp.concatenate(top_bounds, axis=0).astype(BF16)
            for ct in range(4):
                value = tiles(part[slot, ct, pl.ds(512 + k * 128, 128), :])
                s1[step, k, pl.ds(ct * 128, 128), :] = rows_of(encode(value, inverse[ct // 2]))
            message(step, 0, k).start()

    def received(step, level, k, ct, first, count, scale):
        n = 128 >> level
        slot = step % SLOTS
        value = tiles(part[slot, ct, pl.ds(k * 128 + first, count), :])
        return value + decode(tiles(recvs[level][step, k, pl.ds(ct * n + first, count), :]), scale)

    def pass_on(step, level):
        n = 128 >> level
        m = n // 2
        slot = step % SLOTS
        scales = []
        for k in range(STREAMS):
            message(step, level, k).wait()
            theirs = recvs[level][step, k, pl.ds(4 * n, 16), :].astype(F32)
            scale, inverse, fresh = [], [], []
            for t in range(2):
                their = theirs[8 * t : 8 * t + 8]
                bound = bound_above(bounds[slot, k, t] + their)
                bounds[slot, k, t] = bound
                fresh.append(bound)
                scale.append(their * (1.0 / TOP))
                inverse.append(TOP / bound)
            sends[level + 1][step, k, pl.ds(4 * m, 16), :] = jnp.concatenate(fresh, axis=0).astype(BF16)
            for ct in range(4):
                total = received(step, level, k, ct, m, m, scale[ct // 2])
                sends[level + 1][step, k, pl.ds(ct * m, m), :] = rows_of(encode(total, inverse[ct // 2]))
            message(step, level + 1, k).start()
            scales.append(scale)
        for k in range(STREAMS):
            for ct in range(4):
                total = received(step, level, k, ct, 0, m, scales[k][ct // 2])
                part[slot, ct, pl.ds(k * 128, m), :] = rows_of(total)

    def finish(step):
        last = LEVELS - 1
        for k in range(STREAMS):
            message(step, last, k).wait()
            theirs = recvs[last][step, k, pl.ds(64, 16), :].astype(F32)
            scale = [theirs[:8] * (1.0 / TOP), theirs[8:] * (1.0 / TOP)]
            total = [rows_of(received(step, last, k, ct, 0, 16, scale[ct // 2])) for ct in range(4)]
            for c in range(2):
                prod[pl.ds(k * 16, 16), pl.ds(c * 128, 128)] = total[c] * total[2 + c]
        place = (step - 2) % 3
        half = jnp.where(step < 2, step, (step - 2) // 3)
        chip = jnp.where(place == 0, flip_one(x), jnp.where(place == 1, flip_three(x), (x + 2) % 4))
        chip = jnp.where(step < 2, x, chip)
        row = lax.broadcasted_iota(jnp.int32, (256, 64), 0)
        column = lax.broadcasted_iota(jnp.int32, (256, 64), 1)
        query = chip * 16 + (row // 128) * 8 + half * 4 + (row % 128) // RANK
        pick = jnp.where(query == column, 1.0, 0.0).astype(F32)
        sums = jnp.dot(prod[...], pick, precision=lax.Precision.HIGHEST, preferred_element_type=F32)
        out[...] += sums * RANK**-0.5

    out[...] = jnp.zeros_like(out)

    def of_turn(turn):
        step = turn
        fits = turn >= 0
        for idle in reversed(IDLE):
            step = jnp.where(turn > idle, step - 1, step)
            fits = jnp.logical_and(fits, turn != idle)
        return step, jnp.logical_and(fits, step < STEPS)

    def turn_body(turn, carry):
        step, fits = of_turn(turn)

        @pl.when(fits)
        def _():
            arrivals(step)
            multiply(step)

        for level in range(LEVELS - 1):
            step_l, fits_l = of_turn(turn - 1 - level)

            @pl.when(fits_l)
            def _():
                pass_on(step_l, level)

        step_f, fits_f = of_turn(turn - LEVELS)

        @pl.when(fits_f)
        def _():
            finish(step_f)

        return carry

    lax.fori_loop(0, TURNS, turn_body, 0)

    for h in range(2):
        for j in range(8):
            for a in range(2):
                query_copy(a, h, j).wait_send()


def shards(activations, out_grads, query_out, query_in):
    ff, d = activations.shape[1], out_grads.shape[1]
    rows = [4 * (128 >> level) + 16 for level in range(LEVELS)]
    messages = [pltpu.VMEM((STEPS, STREAMS, r, 128), BF16) for r in rows]
    return pl.pallas_call(
        kernel,
        out_shape=jax.ShapeDtypeStruct((64, 64), F32),
        in_specs=[pl.BlockSpec(memory_space=pl.ANY)] * 4,
        out_specs=pl.BlockSpec(memory_space=pltpu.VMEM),
        scratch_shapes=[
            pltpu.VMEM((1024, ff), BF16),
            pltpu.VMEM((1024, d), BF16),
            pltpu.VMEM((STEPS, 2, 128, ff), BF16),
            pltpu.VMEM((STEPS, 2, 128, d), BF16),
            pltpu.VMEM((SLOTS, 4, 1024, 128), F32),
            pltpu.VMEM((SLOTS, STREAMS, 2, 8, 128), F32),
            pltpu.VMEM((64, 256), F32),
            *messages,
            *messages,
            pltpu.SemaphoreType.DMA((2,)),
            pltpu.SemaphoreType.DMA((2, 2)),
            pltpu.SemaphoreType.DMA((2, 2, 8)),
            pltpu.SemaphoreType.DMA((2, 2, 8)),
            pltpu.SemaphoreType.DMA((STEPS, LEVELS, STREAMS)),
            pltpu.SemaphoreType.DMA((STEPS, LEVELS, STREAMS)),
        ],
        compiler_params=pltpu.CompilerParams(
            collective_id=0, has_side_effects=True, vmem_limit_bytes=56 * 1024 * 1024
        ),
    )(
        activations,
        out_grads,
        query_in.reshape(256, ff),
        query_out.reshape(256, d),
    )


def solution(mesh):
    return jax.shard_map(
        shards,
        mesh=mesh,
        in_specs=(
            P("tok", "feat"),
            P("tok", "feat"),
            P("tok", None, "feat"),
            P("tok", None, "feat"),
        ),
        out_specs=P(("tok", "feat"), None),
        check_vma=False,
    )
```

```python
import jax
import jax.numpy as jnp
from jax import lax
from jax.experimental import pallas as pl
from jax.experimental.pallas import tpu as pltpu
from jax.sharding import PartitionSpec as P

RANK = 32
MESH = pl.DeviceIdType.MESH
F32 = jnp.float32
BF16 = jnp.bfloat16

STREAMS = 4
LEVELS = 4
STEPS = 8
LAGS = (1, 2, 3, 4)
SLOTS = 8
POWER = 17
TOP = 2.0 ** (127.0 / POWER)
TINY = 2.0**-100
IDLE = (2,)
TURNS = STEPS + len(IDLE) + LAGS[-1]


def order_of(k):
    return [(k + level) % 4 for level in range(LEVELS)]


def bit(group, d):
    return (group >> (3 - d)) % 2


def kept(k, level):
    return [g for g in range(16) if not any(bit(g, d) for d in order_of(k)[: level + 1])]


def split(k, level):
    held = range(16) if level == 0 else kept(k, level - 1)
    d = order_of(k)[level]
    return [g for g in held if bit(g, d)], [g for g in held if not bit(g, d)]


def rows_at(group, k):
    return pl.ds(group * 64 + k * 16, 16)


def flip_one(v):
    return v + 1 - 2 * (v % 2)


def flip_three(v):
    return 3 - v


def encode(value, inverse):
    n = value * inverse
    n2 = n * n
    n4 = n2 * n2
    n8 = n4 * n4
    return (n8 * n8 * n).astype(BF16)


def decode(sent, scale):
    y = sent.astype(F32)
    log = jnp.log2(jnp.maximum(jnp.abs(y), 2.0**-126))
    return y * jnp.exp2(log * (1.0 / POWER - 1.0)) * scale


def bound_above(bound):
    return jnp.maximum((bound * 1.01).astype(BF16).astype(F32), TINY)


def tiles(value):
    return value.reshape(value.shape[0] // 8, 8, 128)


def rows_of(value):
    return value.reshape(value.shape[0] * 8, 128)


def kernel(
    act, og, qi, qo, out,
    a_v, g_v, qi_v, qo_v, part, bounds, prod,
    s1, s2, s3, s4, r1, r2, r3, r4,
    load_sem, own_sem, sib_send, sib_recv, near_send, near_recv, pass_send, pass_recv,
    relay_send, relay_recv, far_send, far_recv, m_send, m_recv,
):
    tok = lax.axis_index("tok")
    feat = lax.axis_index("feat")
    x, core = tok // 2, tok % 2
    z, y = feat // 4, feat % 4
    sibling = (tok + 1 - 2 * core, feat)
    near_a = (flip_one(x) * 2 + core, feat)
    near_b = (flip_three(x) * 2 + core, feat)
    partners = (
        (tok, z * 4 + flip_one(y)),
        (tok, z * 4 + flip_three(y)),
        (tok, flip_one(z) * 4 + y),
        (tok, flip_three(z) * 4 + y),
    )
    sends, recvs = (s1, s2, s3, s4), (r1, r2, r3, r4)

    barrier = pltpu.get_barrier_semaphore()
    for device in (sibling, near_a, near_b) + partners:
        pl.semaphore_signal(barrier, inc=1, device_id=device, device_id_type=MESH)

    arrays = ((qi, qi_v), (qo, qo_v))

    def own_copy(h, a):
        src, dst = arrays[a]
        return pltpu.make_async_copy(src.at[pl.ds(2 * h, 2)], dst.at[h, pl.ds(2 * core, 2)], own_sem.at[h, a])

    for h in range(2):
        for a in range(2):
            own_copy(h, a).start()
    for group in range(16):
        gy = flip_one(y) if bit(group, 0) else y
        gy = flip_three(gy) if bit(group, 1) else gy
        gz = flip_one(z) if bit(group, 2) else z
        gz = flip_three(gz) if bit(group, 3) else gz
        row = pl.multiple_of((gz * 4 + gy) * 64, 64)
        pltpu.make_async_copy(og.at[pl.ds(row, 64)], g_v.at[pl.ds(group * 64, 64)], load_sem.at[1]).start()
        pltpu.make_async_copy(act.at[pl.ds(row, 64)], a_v.at[pl.ds(group * 64, 64)], load_sem.at[0]).start()

    def remote(src, dst, send, recv, device):
        return pltpu.make_async_remote_copy(src, dst, send, recv, device_id=device, device_id_type=MESH)

    def sibling_copy(h, a):
        src, dst = arrays[a]
        return remote(src.at[pl.ds(2 * h, 2)], dst.at[h, pl.ds(2 * core, 2)], sib_send.at[h, a], sib_recv.at[h, a], sibling)

    def near_copy(q, a, side):
        src, dst = arrays[a]
        return remote(
            src.at[q], dst.at[2 + q, 2 * side + core], near_send.at[q, a, side], near_recv.at[q, a, side], (near_a, near_b)[side]
        )

    def pass_copy(q, a, side):
        place = arrays[a][1].at[2 + q, 2 * side + core]
        return remote(place, place, pass_send.at[q, a, side], pass_recv.at[q, a, side], sibling)

    def relay_copy(q, a, side):
        dst, half = arrays[a][1], pl.ds(32 * side, 32)
        return remote(
            dst.at[2 + q, 2 * side + core, half], dst.at[6 + q // 2, 2 * core + q % 2, half],
            relay_send.at[q, a, side], relay_recv.at[q, a, side], (near_b, near_a)[side],
        )

    def far_copy(h, a):
        place = arrays[a][1].at[6 + h, pl.ds(2 * core, 2)]
        return remote(place, place, far_send.at[h, a], far_recv.at[h, a], sibling)

    pl.semaphore_wait(barrier, 7)
    for q in range(4):
        for side in range(2):
            for a in range(2):
                near_copy(q, a, side).start()
        if q < 2:
            for a in range(2):
                sibling_copy(q, a).start()

    def message(step, level, k):
        return remote(
            sends[level].at[step, k], recvs[level].at[step, k], m_send.at[step, level, k], m_recv.at[step, level, k],
            partners[order_of(k)[level]],
        )

    def hand_over(step):
        for q in range(4):
            @pl.when(step == 2 + q)
            def _():
                for side in range(2):
                    for a in range(2):
                        near_copy(q, a, side).wait_recv()
                        relay_copy(q, a, side).start()
                        pass_copy(q, a, side).start()

        for h in range(2):
            @pl.when(step == 6 + h)
            def _():
                for a in range(2):
                    for q in (2 * h, 2 * h + 1):
                        for side in range(2):
                            relay_copy(q, a, side).wait_recv()
                    far_copy(h, a).start()

    def arrivals(step):
        for h in range(2):
            @pl.when(step == h)
            def _():
                for a in range(2):
                    own_copy(h, a).wait()
                    sibling_copy(h, a).wait_recv()

        for q in range(4):
            @pl.when(step == 2 + q)
            def _():
                for side in range(2):
                    for a in range(2):
                        pass_copy(q, a, side).wait_recv()

        for h in range(2):
            @pl.when(step == 6 + h)
            def _():
                for a in range(2):
                    far_copy(h, a).wait_recv()

        @pl.when(step == 0)
        def _():
            pltpu.make_async_copy(og, g_v, load_sem.at[1]).wait()
            pltpu.make_async_copy(act, a_v, load_sem.at[0]).wait()

    def multiply(step):
        slot = step % SLOTS
        for t, (tokens, queries) in enumerate(((a_v, qi_v), (g_v, qo_v))):
            weights = queries[step].reshape(256, queries.shape[3])
            for m in range(2):
                block = lax.dot_general(
                    tokens[pl.ds(m * 512, 512), :], weights, (((1,), (1,)), ((), ())), preferred_element_type=F32
                )
                part[slot, 2 * t, pl.ds(m * 512, 512), :] = block[:, :128]
                part[slot, 2 * t + 1, pl.ds(m * 512, 512), :] = block[:, 128:]
        inverse, top_bounds = [], []
        for t in range(2):
            top = jnp.max(jnp.abs(part[slot, pl.ds(2 * t, 2)].reshape(256, 8, 128)), axis=0)
            top = jnp.max(jnp.max(top, axis=1, keepdims=True), axis=0, keepdims=True)
            bound = bound_above(jnp.broadcast_to(top, (8, 128)))
            for k in range(STREAMS):
                bounds[slot, k, t] = bound
            top_bounds.append(bound)
            inverse.append(TOP / bound)
        for k in range(STREAMS):
            s1[step, k, pl.ds(512, 16), :] = jnp.concatenate(top_bounds, axis=0).astype(BF16)
            for ct in range(4):
                for i, group in enumerate(split(k, 0)[0]):
                    value = tiles(part[slot, ct, rows_at(group, k), :])
                    s1[step, k, pl.ds(ct * 128 + i * 16, 16), :] = rows_of(encode(value, inverse[ct // 2]))
            message(step, 0, k).start()

    def total_of(step, level, k, ct, group, scale):
        n = 128 >> level
        value = tiles(part[step % SLOTS, ct, rows_at(group, k), :])
        place = pl.ds(ct * n + kept(k, level).index(group) * 16, 16)
        return value + decode(tiles(recvs[level][step, k, place, :]), scale)

    def pass_on(step, level):
        n = 128 >> level
        m = n // 2
        slot = step % SLOTS
        scales = []
        for k in range(STREAMS):
            message(step, level, k).wait()
            theirs = recvs[level][step, k, pl.ds(4 * n, 16), :].astype(F32)
            scale, inverse, fresh = [], [], []
            for t in range(2):
                their = theirs[8 * t : 8 * t + 8]
                bound = bound_above(bounds[slot, k, t] + their)
                bounds[slot, k, t] = bound
                fresh.append(bound)
                scale.append(their * (1.0 / TOP))
                inverse.append(TOP / bound)
            sends[level + 1][step, k, pl.ds(4 * m, 16), :] = jnp.concatenate(fresh, axis=0).astype(BF16)
            for ct in range(4):
                for i, group in enumerate(split(k, level + 1)[0]):
                    total = total_of(step, level, k, ct, group, scale[ct // 2])
                    sends[level + 1][step, k, pl.ds(ct * m + i * 16, 16), :] = rows_of(encode(total, inverse[ct // 2]))
            message(step, level + 1, k).start()
            scales.append(scale)
        for k in range(STREAMS):
            for ct in range(4):
                for group in split(k, level + 1)[1]:
                    total = total_of(step, level, k, ct, group, scales[k][ct // 2])
                    part[slot, ct, rows_at(group, k), :] = rows_of(total)

    def finish(step):
        last = LEVELS - 1
        for k in range(STREAMS):
            message(step, last, k).wait()
            theirs = recvs[last][step, k, pl.ds(64, 16), :].astype(F32)
            scale = [theirs[:8] * (1.0 / TOP), theirs[8:] * (1.0 / TOP)]
            total = [rows_of(total_of(step, last, k, ct, 0, scale[ct // 2])) for ct in range(4)]
            for c in range(2):
                prod[pl.ds(k * 16, 16), pl.ds(c * 128, 128)] = total[c] * total[2 + c]
        row = lax.broadcasted_iota(jnp.int32, (256, 64), 0)
        column = lax.broadcasted_iota(jnp.int32, (256, 64), 1)
        block = row // 64
        near = jnp.logical_and(step >= 2, step < 6)
        chip = jnp.where(step < 2, x, (x + 2) % 4)
        chip = jnp.where(near, jnp.where(block < 2, flip_one(x), flip_three(x)), chip)
        side = jnp.where(near, block % 2, block // 2)
        quarter = jnp.where(near, step - 2, 2 * (step % 2) + block % 2)
        query = chip * 16 + side * 8 + quarter * 2 + (row % 64) // RANK
        pick = jnp.where(query == column, 1.0, 0.0).astype(F32)
        sums = jnp.dot(prod[...], pick, precision=lax.Precision.HIGHEST, preferred_element_type=F32)
        out[...] += sums * RANK**-0.5

    out[...] = jnp.zeros_like(out)

    def of_turn(turn):
        step = turn
        fits = turn >= 0
        for idle in reversed(IDLE):
            step = jnp.where(turn > idle, step - 1, step)
            fits = jnp.logical_and(fits, turn != idle)
        return step, jnp.logical_and(fits, step < STEPS)

    def turn_body(turn, carry):
        step, fits = of_turn(turn)

        @pl.when(fits)
        def _():
            arrivals(step)
            multiply(step)

        for level in range(LEVELS - 1):
            step_l, fits_l = of_turn(turn - LAGS[level])

            @pl.when(fits_l)
            def _():
                pass_on(step_l, level)

        step_f, fits_f = of_turn(turn - LAGS[-1])

        @pl.when(fits_f)
        def _():
            finish(step_f)

        step_n, fits_n = of_turn(turn + 1)

        @pl.when(fits_n)
        def _():
            hand_over(step_n)

        return carry

    lax.fori_loop(0, TURNS, turn_body, 0)

    for a in range(2):
        for h in range(2):
            sibling_copy(h, a).wait_send()
            far_copy(h, a).wait_send()
        for q in range(4):
            for side in range(2):
                near_copy(q, a, side).wait_send()
                pass_copy(q, a, side).wait_send()
                relay_copy(q, a, side).wait_send()


def shards(activations, out_grads, query_out, query_in):
    ff, d = activations.shape[1], out_grads.shape[1]
    rows = [4 * (128 >> level) + 16 for level in range(LEVELS)]
    messages = [pltpu.VMEM((STEPS, STREAMS, r, 128), BF16) for r in rows]
    return pl.pallas_call(
        kernel,
        out_shape=jax.ShapeDtypeStruct((64, 64), F32),
        in_specs=[pl.BlockSpec(memory_space=pl.ANY)] * 4,
        out_specs=pl.BlockSpec(memory_space=pltpu.VMEM),
        scratch_shapes=[
            pltpu.VMEM((1024, ff), BF16),
            pltpu.VMEM((1024, d), BF16),
            pltpu.VMEM((STEPS, 4, 64, ff), BF16),
            pltpu.VMEM((STEPS, 4, 64, d), BF16),
            pltpu.VMEM((SLOTS, 4, 1024, 128), F32),
            pltpu.VMEM((SLOTS, STREAMS, 2, 8, 128), F32),
            pltpu.VMEM((64, 256), F32),
            *messages,
            *messages,
            pltpu.SemaphoreType.DMA((2,)),
            pltpu.SemaphoreType.DMA((2, 2)),
            *[pltpu.SemaphoreType.DMA((2, 2))] * 2,
            *[pltpu.SemaphoreType.DMA((4, 2, 2))] * 6,
            *[pltpu.SemaphoreType.DMA((2, 2))] * 2,
            pltpu.SemaphoreType.DMA((STEPS, LEVELS, STREAMS)),
            pltpu.SemaphoreType.DMA((STEPS, LEVELS, STREAMS)),
        ],
        compiler_params=pltpu.CompilerParams(
            collective_id=0, has_side_effects=True, vmem_limit_bytes=56 * 1024 * 1024
        ),
    )(
        activations,
        out_grads,
        query_in.reshape(4, 64, ff),
        query_out.reshape(4, 64, d),
    )


def solution(mesh):
    return jax.shard_map(
        shards,
        mesh=mesh,
        in_specs=(
            P("tok", "feat"),
            P("tok", "feat"),
            P("tok", None, "feat"),
            P("tok", None, "feat"),
        ),
        out_specs=P(("tok", "feat"), None),
        check_vma=False,
    )
```

```python
import jax
import jax.numpy as jnp
from jax import lax
from jax.experimental import pallas as pl
from jax.experimental.pallas import tpu as pltpu
from jax.sharding import PartitionSpec as P

RANK = 32
MESH = pl.DeviceIdType.MESH
F32 = jnp.float32
BF16 = jnp.bfloat16

STREAMS = 4
LEVELS = 4
STEPS = 8
LAGS = (1, 2, 3, 4)
SLOTS = 8
DIRECT = 7
POWER = 17
TOP = 2.0 ** (127.0 / POWER)
TINY = 2.0**-100
IDLE = ()
AHEAD = 1
TURNS = STEPS + len(IDLE) + LAGS[-2]


def order_of(k):
    return [(k + level) % 4 for level in range(LEVELS)]


def bit(group, d):
    return (group >> (3 - d)) % 2


def kept(k, level):
    return [g for g in range(16) if not any(bit(g, d) for d in order_of(k)[: level + 1])]


def split(k, level):
    held = range(16) if level == 0 else kept(k, level - 1)
    d = order_of(k)[level]
    return [g for g in held if bit(g, d)], [g for g in held if not bit(g, d)]


def last_groups(k):
    third, fourth = order_of(k)[2:]
    return [8 >> third, 8 >> fourth, (8 >> third) + (8 >> fourth)]


def rows_at(group, k):
    return pl.ds(group * 64 + k * 16, 16)


def flip_one(v):
    return v + 1 - 2 * (v % 2)


def flip_three(v):
    return 3 - v


def encode(value, inverse):
    n = value * inverse
    n2 = n * n
    n4 = n2 * n2
    n8 = n4 * n4
    return (n8 * n8 * n).astype(BF16)


def decode(sent, scale):
    y = sent.astype(F32)
    log = jnp.log2(jnp.maximum(jnp.abs(y), 2.0**-126))
    return y * jnp.exp2(log * (1.0 / POWER - 1.0)) * scale


def bound_above(bound):
    return jnp.maximum((bound * 1.01).astype(BF16).astype(F32), TINY)


def tiles(value):
    return value.reshape(value.shape[0] // 8, 8, 128)


def rows_of(value):
    return value.reshape(value.shape[0] * 8, 128)


def kernel(
    act, og, qi, qo, out,
    a_v, g_v, qi_v, qo_v, part, bounds, prod,
    s1, s2, s3, s4, r1, r2, r3, r4, ds, dr,
    load_sem, own_sem, sib_send, sib_recv, near_send, near_recv, pass_send, pass_recv,
    relay_send, relay_recv, far_send, far_recv, m_send, m_recv, d_send, d_recv,
):
    tok = lax.axis_index("tok")
    feat = lax.axis_index("feat")
    x, core = tok // 2, tok % 2
    z, y = feat // 4, feat % 4
    sibling = (tok + 1 - 2 * core, feat)
    near_a = (flip_one(x) * 2 + core, feat)
    near_b = (flip_three(x) * 2 + core, feat)
    partners = (
        (tok, z * 4 + flip_one(y)),
        (tok, z * 4 + flip_three(y)),
        (tok, flip_one(z) * 4 + y),
        (tok, flip_three(z) * 4 + y),
    )
    sends, recvs = (s1, s2, s3, s4), (r1, r2, r3, r4)

    def device_of(group):
        gy = flip_one(y) if bit(group, 0) else y
        gy = flip_three(gy) if bit(group, 1) else gy
        gz = flip_one(z) if bit(group, 2) else z
        gz = flip_three(gz) if bit(group, 3) else gz
        return gz * 4 + gy

    corners = tuple((tok, device_of(last_groups(k)[2])) for k in range(STREAMS))

    barrier = pltpu.get_barrier_semaphore()
    for device in (sibling, near_a, near_b) + partners + corners:
        pl.semaphore_signal(barrier, inc=1, device_id=device, device_id_type=MESH)

    arrays = ((qi, qi_v), (qo, qo_v))

    def own_copy(h, a):
        src, dst = arrays[a]
        return pltpu.make_async_copy(src.at[pl.ds(2 * h, 2)], dst.at[h, pl.ds(2 * core, 2)], own_sem.at[h, a])

    for h in range(2):
        for a in range(2):
            own_copy(h, a).start()
    for group in range(16):
        row = pl.multiple_of(device_of(group) * 64, 64)
        pltpu.make_async_copy(og.at[pl.ds(row, 64)], g_v.at[pl.ds(group * 64, 64)], load_sem.at[1]).start()
        pltpu.make_async_copy(act.at[pl.ds(row, 64)], a_v.at[pl.ds(group * 64, 64)], load_sem.at[0]).start()

    def remote(src, dst, send, recv, device):
        return pltpu.make_async_remote_copy(src, dst, send, recv, device_id=device, device_id_type=MESH)

    def sibling_copy(h, a):
        src, dst = arrays[a]
        return remote(src.at[pl.ds(2 * h, 2)], dst.at[h, pl.ds(2 * core, 2)], sib_send.at[h, a], sib_recv.at[h, a], sibling)

    def near_copy(q, a, side):
        src, dst = arrays[a]
        return remote(
            src.at[q], dst.at[2 + q, 2 * side + core], near_send.at[q, a, side], near_recv.at[q, a, side], (near_a, near_b)[side]
        )

    def pass_copy(q, a, side):
        place = arrays[a][1].at[2 + q, 2 * side + core]
        return remote(place, place, pass_send.at[q, a, side], pass_recv.at[q, a, side], sibling)

    def relay_copy(q, a, side):
        dst, half = arrays[a][1], pl.ds(32 * side, 32)
        return remote(
            dst.at[2 + q, 2 * side + core, half], dst.at[6 + q // 2, 2 * core + q % 2, half],
            relay_send.at[q, a, side], relay_recv.at[q, a, side], (near_b, near_a)[side],
        )

    def far_copy(q, a):
        place = arrays[a][1].at[6 + q // 2, 2 * core + q % 2]
        return remote(place, place, far_send.at[q, a], far_recv.at[q, a], sibling)

    pl.semaphore_wait(barrier, 11)
    for q in range(4):
        for side in range(2):
            for a in range(2):
                near_copy(q, a, side).start()
        if q < 2:
            for a in range(2):
                sibling_copy(q, a).start()

    def message(step, level, k):
        return remote(
            sends[level].at[step, k], recvs[level].at[step, k], m_send.at[step, level, k], m_recv.at[step, level, k],
            partners[order_of(k)[level]],
        )

    def direct(step, k, j):
        return remote(
            ds.at[step - DIRECT, k, j], dr.at[step - DIRECT, k, j], d_send.at[step - DIRECT, k, j], d_recv.at[step - DIRECT, k, j],
            (tok, device_of(last_groups(k)[j])),
        )

    def hand_over_near(step):
        for q in range(4):
            @pl.when(step == 2 + q)
            def _():
                for side in range(2):
                    for a in range(2):
                        near_copy(q, a, side).wait_recv()
                        relay_copy(q, a, side).start()
                        pass_copy(q, a, side).start()

    def hand_over_far(step):
        for h in range(2):
            @pl.when(step == 6 + h)
            def _():
                for q in (2 * h, 2 * h + 1):
                    for a in range(2):
                        for side in range(2):
                            relay_copy(q, a, side).wait_recv()
                        far_copy(q, a).start()

    def arrivals(step):
        for h in range(2):
            @pl.when(step == h)
            def _():
                for a in range(2):
                    own_copy(h, a).wait()
                    sibling_copy(h, a).wait_recv()

        for q in range(4):
            @pl.when(step == 2 + q)
            def _():
                for side in range(2):
                    for a in range(2):
                        pass_copy(q, a, side).wait_recv()

        for h in range(2):
            @pl.when(step == 6 + h)
            def _():
                for a in range(2):
                    for q in (2 * h, 2 * h + 1):
                        far_copy(q, a).wait_recv()

        @pl.when(step == 0)
        def _():
            pltpu.make_async_copy(og, g_v, load_sem.at[1]).wait()
            pltpu.make_async_copy(act, a_v, load_sem.at[0]).wait()

    def multiply(step):
        slot = step % SLOTS
        for t, (tokens, queries) in enumerate(((a_v, qi_v), (g_v, qo_v))):
            weights = queries[step].reshape(256, queries.shape[3])
            for m in range(2):
                block = lax.dot_general(
                    tokens[pl.ds(m * 512, 512), :], weights, (((1,), (1,)), ((), ())), preferred_element_type=F32
                )
                part[slot, 2 * t, pl.ds(m * 512, 512), :] = block[:, :128]
                part[slot, 2 * t + 1, pl.ds(m * 512, 512), :] = block[:, 128:]
        inverse, top_bounds = [], []
        for t in range(2):
            top = jnp.max(jnp.abs(part[slot, pl.ds(2 * t, 2)].reshape(256, 8, 128)), axis=0)
            top = jnp.max(jnp.max(top, axis=1, keepdims=True), axis=0, keepdims=True)
            bound = bound_above(jnp.broadcast_to(top, (8, 128)))
            for k in range(STREAMS):
                bounds[slot, k, t] = bound
            top_bounds.append(bound)
            inverse.append(TOP / bound)
        for k in range(STREAMS):
            s1[step, k, pl.ds(512, 16), :] = jnp.concatenate(top_bounds, axis=0).astype(BF16)
            for ct in range(4):
                for i, group in enumerate(split(k, 0)[0]):
                    value = tiles(part[slot, ct, rows_at(group, k), :])
                    s1[step, k, pl.ds(ct * 128 + i * 16, 16), :] = rows_of(encode(value, inverse[ct // 2]))
            message(step, 0, k).start()

    def total_of(step, level, k, ct, group, scale):
        n = 128 >> level
        value = tiles(part[step % SLOTS, ct, rows_at(group, k), :])
        place = pl.ds(ct * n + kept(k, level).index(group) * 16, 16)
        return value + decode(tiles(recvs[level][step, k, place, :]), scale)

    def pass_on(step, level):
        n = 128 >> level
        m = n // 2
        slot = step % SLOTS
        scales = []
        for k in range(STREAMS):
            message(step, level, k).wait()
            theirs = recvs[level][step, k, pl.ds(4 * n, 16), :].astype(F32)
            scale, inverse, fresh = [], [], []
            for t in range(2):
                their = theirs[8 * t : 8 * t + 8]
                bound = bound_above(bounds[slot, k, t] + their)
                bounds[slot, k, t] = bound
                fresh.append(bound)
                scale.append(their * (1.0 / TOP))
                inverse.append(TOP / bound)
            sends[level + 1][step, k, pl.ds(4 * m, 16), :] = jnp.concatenate(fresh, axis=0).astype(BF16)
            for ct in range(4):
                for i, group in enumerate(split(k, level + 1)[0]):
                    total = total_of(step, level, k, ct, group, scale[ct // 2])
                    sends[level + 1][step, k, pl.ds(ct * m + i * 16, 16), :] = rows_of(encode(total, inverse[ct // 2]))
            message(step, level + 1, k).start()
            scales.append(scale)
        for k in range(STREAMS):
            for ct in range(4):
                for group in split(k, level + 1)[1]:
                    total = total_of(step, level, k, ct, group, scales[k][ct // 2])
                    part[slot, ct, rows_at(group, k), :] = rows_of(total)

    def next_bounds(step, k, theirs):
        scale, inverse, fresh = [], [], []
        for t in range(2):
            their = theirs[8 * t : 8 * t + 8]
            bound = bound_above(bounds[step % SLOTS, k, t] + their)
            fresh.append(bound)
            scale.append(their * (1.0 / TOP))
            inverse.append(TOP / bound)
        return scale, inverse, jnp.concatenate(fresh, axis=0).astype(BF16)

    def spread(step):
        level, slot = 1, step % SLOTS
        scales = []
        for k in range(STREAMS):
            message(step, level, k).wait()
            theirs = recvs[level][step, k, pl.ds(4 * 64, 16), :].astype(F32)
            scale, inverse, fresh = next_bounds(step, k, theirs)
            for j, group in enumerate(last_groups(k)):
                ds[step - DIRECT, k, j, pl.ds(64, 16), :] = fresh
                for ct in range(4):
                    total = total_of(step, level, k, ct, group, scale[ct // 2])
                    ds[step - DIRECT, k, j, pl.ds(ct * 16, 16), :] = rows_of(encode(total, inverse[ct // 2]))
                direct(step, k, j).start()
            scales.append(scale)
        for k in range(STREAMS):
            for ct in range(4):
                total = total_of(step, level, k, ct, 0, scales[k][ct // 2])
                part[slot, ct, rows_at(0, k), :] = rows_of(total)

    def finish(step):
        last = LEVELS - 1
        for k in range(STREAMS):
            message(step, last, k).wait()
            theirs = recvs[last][step, k, pl.ds(64, 16), :].astype(F32)
            scale = [theirs[:8] * (1.0 / TOP), theirs[8:] * (1.0 / TOP)]
            total = [rows_of(total_of(step, last, k, ct, 0, scale[ct // 2])) for ct in range(4)]
            for c in range(2):
                prod[pl.ds(k * 16, 16), pl.ds(c * 128, 128)] = total[c] * total[2 + c]
        add_scores(step)

    def finish_direct(step):
        for k in range(STREAMS):
            total = [tiles(part[step % SLOTS, ct, rows_at(0, k), :]) for ct in range(4)]
            for j in range(3):
                direct(step, k, j).wait()
                theirs = dr[step - DIRECT, k, j, pl.ds(64, 16), :].astype(F32)
                scale = [theirs[:8] * (1.0 / TOP), theirs[8:] * (1.0 / TOP)]
                for ct in range(4):
                    total[ct] += decode(tiles(dr[step - DIRECT, k, j, pl.ds(ct * 16, 16), :]), scale[ct // 2])
            for c in range(2):
                prod[pl.ds(k * 16, 16), pl.ds(c * 128, 128)] = rows_of(total[c] * total[2 + c])
        add_scores(step)

    def add_scores(step):
        row = lax.broadcasted_iota(jnp.int32, (256, 64), 0)
        column = lax.broadcasted_iota(jnp.int32, (256, 64), 1)
        block = row // 64
        near = jnp.logical_and(step >= 2, step < 6)
        chip = jnp.where(step < 2, x, (x + 2) % 4)
        chip = jnp.where(near, jnp.where(block < 2, flip_one(x), flip_three(x)), chip)
        side = jnp.where(near, block % 2, block // 2)
        quarter = jnp.where(near, step - 2, 2 * (step % 2) + block % 2)
        query = chip * 16 + side * 8 + quarter * 2 + (row % 64) // RANK
        pick = jnp.where(query == column, 1.0, 0.0).astype(F32)
        sums = jnp.dot(prod[...], pick, precision=lax.Precision.HIGHEST, preferred_element_type=F32)
        out[...] += sums * RANK**-0.5

    out[...] = jnp.zeros_like(out)

    def of_turn(turn):
        step = turn
        fits = turn >= 0
        for idle in reversed(IDLE):
            step = jnp.where(turn > idle, step - 1, step)
            fits = jnp.logical_and(fits, turn != idle)
        return step, jnp.logical_and(fits, step < STEPS)

    def turn_body(turn, carry):
        step, fits = of_turn(turn)

        @pl.when(fits)
        def _():
            arrivals(step)
            multiply(step)

        step_0, fits_0 = of_turn(turn - LAGS[0])

        @pl.when(fits_0)
        def _():
            pass_on(step_0, 0)

        step_n, fits_n = of_turn(turn + AHEAD)

        @pl.when(fits_n)
        def _():
            hand_over_near(step_n)

        step_1, fits_1 = of_turn(turn - LAGS[1])

        @pl.when(jnp.logical_and(fits_1, step_1 < DIRECT))
        def _():
            pass_on(step_1, 1)

        @pl.when(jnp.logical_and(fits_1, step_1 >= DIRECT))
        def _():
            spread(step_1)

        step_o, fits_o = of_turn(turn + 1)

        @pl.when(fits_o)
        def _():
            hand_over_far(step_o)

        step_2, fits_2 = of_turn(turn - LAGS[2])

        @pl.when(jnp.logical_and(fits_2, step_2 < DIRECT))
        def _():
            pass_on(step_2, 2)

        step_3, fits_3 = of_turn(turn - LAGS[3])

        @pl.when(jnp.logical_and(fits_3, step_3 < DIRECT))
        def _():
            finish(step_3)

        @pl.when(jnp.logical_and(fits_2, step_2 >= DIRECT))
        def _():
            finish_direct(step_2)

        return carry

    lax.fori_loop(0, TURNS, turn_body, 0)

    for a in range(2):
        for h in range(2):
            sibling_copy(h, a).wait_send()
        for q in range(4):
            far_copy(q, a).wait_send()
            for side in range(2):
                near_copy(q, a, side).wait_send()
                pass_copy(q, a, side).wait_send()
                relay_copy(q, a, side).wait_send()


def shards(activations, out_grads, query_out, query_in):
    ff, d = activations.shape[1], out_grads.shape[1]
    rows = [4 * (128 >> level) + 16 for level in range(LEVELS)]
    messages = [pltpu.VMEM((STEPS, STREAMS, r, 128), BF16) for r in rows]
    return pl.pallas_call(
        kernel,
        out_shape=jax.ShapeDtypeStruct((64, 64), F32),
        in_specs=[pl.BlockSpec(memory_space=pl.ANY)] * 4,
        out_specs=pl.BlockSpec(memory_space=pltpu.VMEM),
        scratch_shapes=[
            pltpu.VMEM((1024, ff), BF16),
            pltpu.VMEM((1024, d), BF16),
            pltpu.VMEM((STEPS, 4, 64, ff), BF16),
            pltpu.VMEM((STEPS, 4, 64, d), BF16),
            pltpu.VMEM((SLOTS, 4, 1024, 128), F32),
            pltpu.VMEM((SLOTS, STREAMS, 2, 8, 128), F32),
            pltpu.VMEM((64, 256), F32),
            *messages,
            *messages,
            *[pltpu.VMEM((STEPS - DIRECT, STREAMS, 3, 80, 128), BF16)] * 2,
            pltpu.SemaphoreType.DMA((2,)),
            pltpu.SemaphoreType.DMA((2, 2)),
            *[pltpu.SemaphoreType.DMA((2, 2))] * 2,
            *[pltpu.SemaphoreType.DMA((4, 2, 2))] * 6,
            *[pltpu.SemaphoreType.DMA((4, 2))] * 2,
            *[pltpu.SemaphoreType.DMA((STEPS, LEVELS, STREAMS))] * 2,
            *[pltpu.SemaphoreType.DMA((STEPS - DIRECT, STREAMS, 3))] * 2,
        ],
        compiler_params=pltpu.CompilerParams(
            collective_id=0, has_side_effects=True, vmem_limit_bytes=56 * 1024 * 1024
        ),
    )(
        activations,
        out_grads,
        query_in.reshape(4, 64, ff),
        query_out.reshape(4, 64, d),
    )


def solution(mesh):
    return jax.shard_map(
        shards,
        mesh=mesh,
        in_specs=(
            P("tok", "feat"),
            P("tok", "feat"),
            P("tok", None, "feat"),
            P("tok", None, "feat"),
        ),
        out_specs=P(("tok", "feat"), None),
        check_vma=False,
    )
```

```python
import jax
import jax.numpy as jnp
from jax import lax
from jax.experimental import pallas as pl
from jax.experimental.pallas import tpu as pltpu
from jax.sharding import PartitionSpec as P

RANK = 32
MESH = pl.DeviceIdType.MESH
F32 = jnp.float32
BF16 = jnp.bfloat16

STREAMS = 4
LEVELS = 4
STEPS = 8
LAGS = (1, 2, 3, 4)
SLOTS = 8
DIRECT = 7
POWER = 17
TOP = 2.0 ** (127.0 / POWER)
TINY = 2.0**-100
IDLE = ()
AHEAD = 1
TURNS = STEPS + len(IDLE) + LAGS[-2]


def order_of(k):
    return [(k + level) % 4 for level in range(LEVELS)]


def bit(group, d):
    return (group >> (3 - d)) % 2


def kept(k, level):
    return [g for g in range(16) if not any(bit(g, d) for d in order_of(k)[: level + 1])]


def split(k, level):
    held = range(16) if level == 0 else kept(k, level - 1)
    d = order_of(k)[level]
    return [g for g in held if bit(g, d)], [g for g in held if not bit(g, d)]


def last_groups(k):
    third, fourth = order_of(k)[2:]
    return [8 >> third, 8 >> fourth, (8 >> third) + (8 >> fourth)]


def rows_at(group, k):
    return pl.ds(group * 64 + k * 16, 16)


def flip_one(v):
    return v + 1 - 2 * (v % 2)


def flip_three(v):
    return 3 - v


def encode(value, inverse):
    n = value * inverse
    n2 = n * n
    n4 = n2 * n2
    n8 = n4 * n4
    return (n8 * n8 * n).astype(BF16)


def decode(sent, scale):
    y = sent.astype(F32)
    log = jnp.log2(jnp.maximum(jnp.abs(y), 2.0**-126))
    return y * jnp.exp2(log * (1.0 / POWER - 1.0)) * scale


def bound_above(bound):
    return jnp.maximum((bound * 1.01).astype(BF16).astype(F32), TINY)


def tiles(value):
    return value.reshape(value.shape[0] // 8, 8, 128)


def rows_of(value):
    return value.reshape(value.shape[0] * 8, 128)


def kernel(
    act, og, qi, qo, out,
    a_v, g_v, qi_v, qo_v, part, bounds, prod,
    s1, s2, s3, s4, r1, r2, r3, r4, ds, dr,
    load_sem, own_sem, sib_send, sib_recv, near_send, near_recv, pass_send, pass_recv,
    relay_send, relay_recv, far_send, far_recv, m_send, m_recv, d_send, d_recv,
):
    tok = lax.axis_index("tok")
    feat = lax.axis_index("feat")
    x, core = tok // 2, tok % 2
    z, y = feat // 4, feat % 4
    sibling = (tok + 1 - 2 * core, feat)
    near_a = (flip_one(x) * 2 + core, feat)
    near_b = (flip_three(x) * 2 + core, feat)
    partners = (
        (tok, z * 4 + flip_one(y)),
        (tok, z * 4 + flip_three(y)),
        (tok, flip_one(z) * 4 + y),
        (tok, flip_three(z) * 4 + y),
    )
    sends, recvs = (s1, s2, s3, s4), (r1, r2, r3, r4)

    def device_of(group):
        gy = flip_one(y) if bit(group, 0) else y
        gy = flip_three(gy) if bit(group, 1) else gy
        gz = flip_one(z) if bit(group, 2) else z
        gz = flip_three(gz) if bit(group, 3) else gz
        return gz * 4 + gy

    corners = tuple((tok, device_of(last_groups(k)[2])) for k in range(STREAMS))

    barrier = pltpu.get_barrier_semaphore()
    for device in (sibling, near_a, near_b) + partners + corners:
        pl.semaphore_signal(barrier, inc=1, device_id=device, device_id_type=MESH)

    arrays = ((qi, qi_v), (qo, qo_v))

    def own_copy(h, a):
        src, dst = arrays[a]
        return pltpu.make_async_copy(src.at[pl.ds(2 * h, 2)], dst.at[0, pl.ds(2 * h, 2)], own_sem.at[h, a])

    for h in range(2):
        for a in range(2):
            own_copy(h, a).start()
    for group in range(16):
        row = pl.multiple_of(device_of(group) * 64, 64)
        pltpu.make_async_copy(og.at[pl.ds(row, 64)], g_v.at[pl.ds(group * 64, 64)], load_sem.at[1]).start()
        pltpu.make_async_copy(act.at[pl.ds(row, 64)], a_v.at[pl.ds(group * 64, 64)], load_sem.at[0]).start()

    def remote(src, dst, send, recv, device):
        return pltpu.make_async_remote_copy(src, dst, send, recv, device_id=device, device_id_type=MESH)

    def sibling_copy(h, a):
        src, dst = arrays[a]
        return remote(src.at[pl.ds(2 * h, 2)], dst.at[1, pl.ds(2 * h, 2)], sib_send.at[h, a], sib_recv.at[h, a], sibling)

    def near_copy(q, a, side):
        src, dst = arrays[a]
        return remote(
            src.at[q], dst.at[2 + q, 2 * side + core], near_send.at[q, a, side], near_recv.at[q, a, side], (near_a, near_b)[side]
        )

    def pass_copy(q, a, side):
        place = arrays[a][1].at[2 + q, 2 * side + core]
        return remote(place, place, pass_send.at[q, a, side], pass_recv.at[q, a, side], sibling)

    def relay_copy(q, a, side):
        dst, half = arrays[a][1], pl.ds(32 * side, 32)
        return remote(
            dst.at[2 + q, 2 * side + core, half], dst.at[6 + q // 2, 2 * core + q % 2, half],
            relay_send.at[q, a, side], relay_recv.at[q, a, side], (near_b, near_a)[side],
        )

    def far_copy(q, a):
        place = arrays[a][1].at[6 + q // 2, 2 * core + q % 2]
        return remote(place, place, far_send.at[q, a], far_recv.at[q, a], sibling)

    pl.semaphore_wait(barrier, 11)
    for q in range(4):
        for side in range(2):
            for a in range(2):
                near_copy(q, a, side).start()
        if q < 2:
            for a in range(2):
                sibling_copy(q, a).start()

    def message(step, level, k):
        return remote(
            sends[level].at[step, k], recvs[level].at[step, k], m_send.at[step, level, k], m_recv.at[step, level, k],
            partners[order_of(k)[level]],
        )

    def direct(step, k, j):
        return remote(
            ds.at[step - DIRECT, k, j], dr.at[step - DIRECT, k, j], d_send.at[step - DIRECT, k, j], d_recv.at[step - DIRECT, k, j],
            (tok, device_of(last_groups(k)[j])),
        )

    def hand_over_near(step):
        for q in range(4):
            @pl.when(step == 2 + q)
            def _():
                for side in range(2):
                    for a in range(2):
                        near_copy(q, a, side).wait_recv()
                        relay_copy(q, a, side).start()
                        pass_copy(q, a, side).start()

    def hand_over_far(step):
        for h in range(2):
            @pl.when(step == 6 + h)
            def _():
                for q in (2 * h, 2 * h + 1):
                    for a in range(2):
                        for side in range(2):
                            relay_copy(q, a, side).wait_recv()
                        far_copy(q, a).start()

    def arrivals(step):
        @pl.when(step == 0)
        def _():
            for h in range(2):
                for a in range(2):
                    own_copy(h, a).wait()

        @pl.when(step == 1)
        def _():
            for h in range(2):
                for a in range(2):
                    sibling_copy(h, a).wait_recv()

        for q in range(4):
            @pl.when(step == 2 + q)
            def _():
                for side in range(2):
                    for a in range(2):
                        pass_copy(q, a, side).wait_recv()

        for h in range(2):
            @pl.when(step == 6 + h)
            def _():
                for a in range(2):
                    for q in (2 * h, 2 * h + 1):
                        far_copy(q, a).wait_recv()

        @pl.when(step == 0)
        def _():
            pltpu.make_async_copy(og, g_v, load_sem.at[1]).wait()
            pltpu.make_async_copy(act, a_v, load_sem.at[0]).wait()

    def multiply(step):
        slot = step % SLOTS
        for t, (tokens, queries) in enumerate(((a_v, qi_v), (g_v, qo_v))):
            weights = queries[step].reshape(256, queries.shape[3])
            for m in range(2):
                block = lax.dot_general(
                    tokens[pl.ds(m * 512, 512), :], weights, (((1,), (1,)), ((), ())), preferred_element_type=F32
                )
                part[slot, 2 * t, pl.ds(m * 512, 512), :] = block[:, :128]
                part[slot, 2 * t + 1, pl.ds(m * 512, 512), :] = block[:, 128:]
        inverse, top_bounds = [], []
        for t in range(2):
            top = jnp.max(jnp.abs(part[slot, pl.ds(2 * t, 2)].reshape(256, 8, 128)), axis=0)
            top = jnp.max(jnp.max(top, axis=1, keepdims=True), axis=0, keepdims=True)
            bound = bound_above(jnp.broadcast_to(top, (8, 128)))
            for k in range(STREAMS):
                bounds[slot, k, t] = bound
            top_bounds.append(bound)
            inverse.append(TOP / bound)
        for k in range(STREAMS):
            s1[step, k, pl.ds(512, 16), :] = jnp.concatenate(top_bounds, axis=0).astype(BF16)
            for ct in range(4):
                for i, group in enumerate(split(k, 0)[0]):
                    value = tiles(part[slot, ct, rows_at(group, k), :])
                    s1[step, k, pl.ds(ct * 128 + i * 16, 16), :] = rows_of(encode(value, inverse[ct // 2]))
            message(step, 0, k).start()

    def total_of(step, level, k, ct, group, scale):
        n = 128 >> level
        value = tiles(part[step % SLOTS, ct, rows_at(group, k), :])
        place = pl.ds(ct * n + kept(k, level).index(group) * 16, 16)
        return value + decode(tiles(recvs[level][step, k, place, :]), scale)

    def pass_on(step, level):
        n = 128 >> level
        m = n // 2
        slot = step % SLOTS
        scales = []
        for k in range(STREAMS):
            message(step, level, k).wait()
            theirs = recvs[level][step, k, pl.ds(4 * n, 16), :].astype(F32)
            scale, inverse, fresh = [], [], []
            for t in range(2):
                their = theirs[8 * t : 8 * t + 8]
                bound = bound_above(bounds[slot, k, t] + their)
                bounds[slot, k, t] = bound
                fresh.append(bound)
                scale.append(their * (1.0 / TOP))
                inverse.append(TOP / bound)
            sends[level + 1][step, k, pl.ds(4 * m, 16), :] = jnp.concatenate(fresh, axis=0).astype(BF16)
            for ct in range(4):
                for i, group in enumerate(split(k, level + 1)[0]):
                    total = total_of(step, level, k, ct, group, scale[ct // 2])
                    sends[level + 1][step, k, pl.ds(ct * m + i * 16, 16), :] = rows_of(encode(total, inverse[ct // 2]))
            message(step, level + 1, k).start()
            scales.append(scale)
        for k in range(STREAMS):
            for ct in range(4):
                for group in split(k, level + 1)[1]:
                    total = total_of(step, level, k, ct, group, scales[k][ct // 2])
                    part[slot, ct, rows_at(group, k), :] = rows_of(total)

    def choice_of(step):
        row = lax.broadcasted_iota(jnp.int32, (256, 64), 0)
        column = lax.broadcasted_iota(jnp.int32, (256, 64), 1)
        block = row // 64
        near = jnp.logical_and(step >= 2, step < 6)
        chip = jnp.where(step < 2, x, (x + 2) % 4)
        chip = jnp.where(near, jnp.where(block < 2, flip_one(x), flip_three(x)), chip)
        side = jnp.where(near, block % 2, block // 2)
        side = jnp.where(step < 2, jnp.where(step == 0, core, 1 - core), side)
        quarter = jnp.where(near, step - 2, 2 * (step % 2) + block % 2)
        quarter = jnp.where(step < 2, block, quarter)
        query = chip * 16 + side * 8 + quarter * 2 + (row % 64) // RANK
        return jnp.where(query == column, 1.0, 0.0).astype(F32)

    def add_scores(choice):
        sums = jnp.dot(prod[...], choice, precision=lax.Precision.HIGHEST, preferred_element_type=F32)
        out[...] += sums * RANK**-0.5

    def next_bounds(step, k, theirs):
        scale, inverse, fresh = [], [], []
        for t in range(2):
            their = theirs[8 * t : 8 * t + 8]
            bound = bound_above(bounds[step % SLOTS, k, t] + their)
            fresh.append(bound)
            scale.append(their * (1.0 / TOP))
            inverse.append(TOP / bound)
        return scale, inverse, jnp.concatenate(fresh, axis=0).astype(BF16)

    def spread(step):
        level, slot = 1, step % SLOTS
        scales = []
        for k in range(STREAMS):
            message(step, level, k).wait()
            theirs = recvs[level][step, k, pl.ds(4 * 64, 16), :].astype(F32)
            scale, inverse, fresh = next_bounds(step, k, theirs)
            for j, group in enumerate(last_groups(k)):
                ds[step - DIRECT, k, j, pl.ds(64, 16), :] = fresh
                for ct in range(4):
                    total = total_of(step, level, k, ct, group, scale[ct // 2])
                    ds[step - DIRECT, k, j, pl.ds(ct * 16, 16), :] = rows_of(encode(total, inverse[ct // 2]))
                direct(step, k, j).start()
            scales.append(scale)
        for k in range(STREAMS):
            for ct in range(4):
                total = total_of(step, level, k, ct, 0, scales[k][ct // 2])
                part[slot, ct, rows_at(0, k), :] = rows_of(total)

    def finish(step):
        choice = choice_of(step)
        last = LEVELS - 1
        for k in range(STREAMS):
            message(step, last, k).wait()
            theirs = recvs[last][step, k, pl.ds(64, 16), :].astype(F32)
            scale = [theirs[:8] * (1.0 / TOP), theirs[8:] * (1.0 / TOP)]
            total = [rows_of(total_of(step, last, k, ct, 0, scale[ct // 2])) for ct in range(4)]
            for c in range(2):
                prod[pl.ds(k * 16, 16), pl.ds(c * 128, 128)] = total[c] * total[2 + c]
        add_scores(choice)

    def finish_direct(step):
        choice = choice_of(step)
        for k in range(STREAMS):
            total = [tiles(part[step % SLOTS, ct, rows_at(0, k), :]) for ct in range(4)]
            for j in range(3):
                direct(step, k, j).wait()
                theirs = dr[step - DIRECT, k, j, pl.ds(64, 16), :].astype(F32)
                scale = [theirs[:8] * (1.0 / TOP), theirs[8:] * (1.0 / TOP)]
                for ct in range(4):
                    total[ct] += decode(tiles(dr[step - DIRECT, k, j, pl.ds(ct * 16, 16), :]), scale[ct // 2])
            for c in range(2):
                prod[pl.ds(k * 16, 16), pl.ds(c * 128, 128)] = rows_of(total[c] * total[2 + c])
        add_scores(choice)

    out[...] = jnp.zeros_like(out)

    def queries_sent():
        for a in range(2):
            for h in range(2):
                sibling_copy(h, a).wait_send()
            for q in range(4):
                far_copy(q, a).wait_send()
                for side in range(2):
                    near_copy(q, a, side).wait_send()
                    pass_copy(q, a, side).wait_send()
                    relay_copy(q, a, side).wait_send()

    def of_turn(turn):
        step = turn
        fits = turn >= 0
        for idle in reversed(IDLE):
            step = jnp.where(turn > idle, step - 1, step)
            fits = jnp.logical_and(fits, turn != idle)
        return step, jnp.logical_and(fits, step < STEPS)

    def turn_body(turn, carry):
        step, fits = of_turn(turn)

        @pl.when(fits)
        def _():
            arrivals(step)
            multiply(step)

        @pl.when(turn == STEPS + len(IDLE))
        def _():
            queries_sent()

        step_n, fits_n = of_turn(turn + AHEAD)

        @pl.when(fits_n)
        def _():
            hand_over_near(step_n)

        step_0, fits_0 = of_turn(turn - LAGS[0])

        @pl.when(fits_0)
        def _():
            pass_on(step_0, 0)

        step_o, fits_o = of_turn(turn + 1)

        @pl.when(fits_o)
        def _():
            hand_over_far(step_o)

        step_1, fits_1 = of_turn(turn - LAGS[1])

        @pl.when(jnp.logical_and(fits_1, step_1 < DIRECT))
        def _():
            pass_on(step_1, 1)

        @pl.when(jnp.logical_and(fits_1, step_1 >= DIRECT))
        def _():
            spread(step_1)

        step_2, fits_2 = of_turn(turn - LAGS[2])

        @pl.when(jnp.logical_and(fits_2, step_2 < DIRECT))
        def _():
            pass_on(step_2, 2)

        step_3, fits_3 = of_turn(turn - LAGS[3])

        @pl.when(jnp.logical_and(fits_3, step_3 < DIRECT))
        def _():
            finish(step_3)

        @pl.when(jnp.logical_and(fits_2, step_2 >= DIRECT))
        def _():
            finish_direct(step_2)

        return carry

    lax.fori_loop(0, TURNS, turn_body, 0)


def shards(activations, out_grads, query_out, query_in):
    ff, d = activations.shape[1], out_grads.shape[1]
    rows = [4 * (128 >> level) + 16 for level in range(LEVELS)]
    messages = [pltpu.VMEM((STEPS, STREAMS, r, 128), BF16) for r in rows]
    return pl.pallas_call(
        kernel,
        out_shape=pltpu.VMEM((64, 64), F32),
        in_specs=[pl.BlockSpec(memory_space=pl.ANY)] * 4,
        out_specs=pl.BlockSpec(memory_space=pltpu.VMEM),
        scratch_shapes=[
            pltpu.VMEM((1024, ff), BF16),
            pltpu.VMEM((1024, d), BF16),
            pltpu.VMEM((STEPS, 4, 64, ff), BF16),
            pltpu.VMEM((STEPS, 4, 64, d), BF16),
            pltpu.VMEM((SLOTS, 4, 1024, 128), F32),
            pltpu.VMEM((SLOTS, STREAMS, 2, 8, 128), F32),
            pltpu.VMEM((64, 256), F32),
            *messages,
            *messages,
            *[pltpu.VMEM((STEPS - DIRECT, STREAMS, 3, 80, 128), BF16)] * 2,
            pltpu.SemaphoreType.DMA((2,)),
            pltpu.SemaphoreType.DMA((2, 2)),
            *[pltpu.SemaphoreType.DMA((2, 2))] * 2,
            *[pltpu.SemaphoreType.DMA((4, 2, 2))] * 6,
            *[pltpu.SemaphoreType.DMA((4, 2))] * 2,
            *[pltpu.SemaphoreType.DMA((STEPS, LEVELS, STREAMS))] * 2,
            *[pltpu.SemaphoreType.DMA((STEPS - DIRECT, STREAMS, 3))] * 2,
        ],
        compiler_params=pltpu.CompilerParams(
            collective_id=0, has_side_effects=True, vmem_limit_bytes=56 * 1024 * 1024
        ),
    )(
        activations,
        out_grads,
        query_in.reshape(4, 64, ff),
        query_out.reshape(4, 64, d),
    )


def solution(mesh):
    return jax.shard_map(
        shards,
        mesh=mesh,
        in_specs=(
            P("tok", "feat"),
            P("tok", "feat"),
            P("tok", None, "feat"),
            P("tok", None, "feat"),
        ),
        out_specs=P(("tok", "feat"), None),
        check_vma=False,
    )
```

```python
import jax
import jax.numpy as jnp
from jax import lax
from jax.experimental import pallas as pl
from jax.experimental.pallas import tpu as pltpu
from jax.sharding import PartitionSpec as P

RANK = 32
MESH = pl.DeviceIdType.MESH
F32 = jnp.float32
BF16 = jnp.bfloat16

STREAMS = 4
LEVELS = 4
STEPS = 8
LAGS = (1, 2, 3, 4)
SLOTS = 8
DIRECT = 7
POWER = 17
TOP = 2.0 ** (127.0 / POWER)
TINY = 2.0**-100
IDLE = ()
AHEAD = 1
TURNS = STEPS + len(IDLE) + LAGS[-2]


def order_of(k):
    return [(k + level) % 4 for level in range(LEVELS)]


def bit(group, d):
    return (group >> (3 - d)) % 2


def kept(k, level):
    return [g for g in range(16) if not any(bit(g, d) for d in order_of(k)[: level + 1])]


def split(k, level):
    held = range(16) if level == 0 else kept(k, level - 1)
    d = order_of(k)[level]
    return [g for g in held if bit(g, d)], [g for g in held if not bit(g, d)]


def last_groups(k):
    third, fourth = order_of(k)[2:]
    return [8 >> third, 8 >> fourth, (8 >> third) + (8 >> fourth)]


def streams_at(level):
    return sorted(range(STREAMS), key=lambda k: order_of(k)[level] % 2)


def rows_at(group, k):
    return pl.ds(group * 64 + k * 16, 16)


def flip_one(v):
    return v + 1 - 2 * (v % 2)


def flip_three(v):
    return 3 - v


def encode(value, inverse):
    n = value * inverse
    n2 = n * n
    n4 = n2 * n2
    n8 = n4 * n4
    return (n8 * n8 * n).astype(BF16)


def decode(sent, scale):
    y = sent.astype(F32)
    log = jnp.log2(jnp.maximum(jnp.abs(y), 2.0**-126))
    return y * jnp.exp2(log * (1.0 / POWER - 1.0)) * scale


def bound_above(bound):
    return jnp.maximum((bound * 1.01).astype(BF16).astype(F32), TINY)


def tiles(value):
    return value.reshape(value.shape[0] // 8, 8, 128)


def rows_of(value):
    return value.reshape(value.shape[0] * 8, 128)


def kernel(
    act, og, qi, qo, out,
    a_v, g_v, qi_v, qo_v, part, bounds, prod,
    s1, s2, s3, s4, r1, r2, r3, r4, ds, dr,
    load_sem, own_sem, sib_send, sib_recv, near_send, near_recv, pass_send, pass_recv,
    relay_send, relay_recv, far_send, far_recv, m_send, m_recv, d_send, d_recv,
):
    tok = lax.axis_index("tok")
    feat = lax.axis_index("feat")
    x, core = tok // 2, tok % 2
    z, y = feat // 4, feat % 4
    sibling = (tok + 1 - 2 * core, feat)
    near_a = (flip_one(x) * 2 + core, feat)
    near_b = (flip_three(x) * 2 + core, feat)
    partners = (
        (tok, z * 4 + flip_one(y)),
        (tok, z * 4 + flip_three(y)),
        (tok, flip_one(z) * 4 + y),
        (tok, flip_three(z) * 4 + y),
    )
    sends, recvs = (s1, s2, s3, s4), (r1, r2, r3, r4)

    def device_of(group):
        gy = flip_one(y) if bit(group, 0) else y
        gy = flip_three(gy) if bit(group, 1) else gy
        gz = flip_one(z) if bit(group, 2) else z
        gz = flip_three(gz) if bit(group, 3) else gz
        return gz * 4 + gy

    corners = tuple((tok, device_of(last_groups(k)[2])) for k in range(STREAMS))

    barrier = pltpu.get_barrier_semaphore()
    for device in (sibling, near_a, near_b) + partners + corners:
        pl.semaphore_signal(barrier, inc=1, device_id=device, device_id_type=MESH)

    arrays = ((qi, qi_v), (qo, qo_v))

    def own_copy(h, a):
        src, dst = arrays[a]
        return pltpu.make_async_copy(src.at[pl.ds(2 * h, 2)], dst.at[0, pl.ds(2 * h, 2)], own_sem.at[h, a])

    for h in range(2):
        for a in range(2):
            own_copy(h, a).start()
    for group in range(16):
        row = pl.multiple_of(device_of(group) * 64, 64)
        pltpu.make_async_copy(og.at[pl.ds(row, 64)], g_v.at[pl.ds(group * 64, 64)], load_sem.at[1]).start()
        pltpu.make_async_copy(act.at[pl.ds(row, 64)], a_v.at[pl.ds(group * 64, 64)], load_sem.at[0]).start()

    def remote(src, dst, send, recv, device):
        return pltpu.make_async_remote_copy(src, dst, send, recv, device_id=device, device_id_type=MESH)

    def sibling_copy(h, a):
        src, dst = arrays[a]
        return remote(src.at[pl.ds(2 * h, 2)], dst.at[1, pl.ds(2 * h, 2)], sib_send.at[h, a], sib_recv.at[h, a], sibling)

    def near_copy(q, a, side):
        src, dst = arrays[a]
        return remote(
            src.at[q], dst.at[2 + q, 2 * side + core], near_send.at[q, a, side], near_recv.at[q, a, side], (near_a, near_b)[side]
        )

    def pass_copy(q, a, side):
        place = arrays[a][1].at[2 + q, 2 * side + core]
        return remote(place, place, pass_send.at[q, a, side], pass_recv.at[q, a, side], sibling)

    def relay_copy(q, a, side):
        dst, half = arrays[a][1], pl.ds(32 * side, 32)
        return remote(
            dst.at[2 + q, 2 * side + core, half], dst.at[6 + q // 2, 2 * core + q % 2, half],
            relay_send.at[q, a, side], relay_recv.at[q, a, side], (near_b, near_a)[side],
        )

    def far_copy(q, a):
        place = arrays[a][1].at[6 + q // 2, 2 * core + q % 2]
        return remote(place, place, far_send.at[q, a], far_recv.at[q, a], sibling)

    pl.semaphore_wait(barrier, 11)
    for q in range(4):
        for side in range(2):
            for a in range(2):
                near_copy(q, a, side).start()
        if q < 2:
            for a in range(2):
                sibling_copy(q, a).start()

    def message(step, level, k):
        return remote(
            sends[level].at[step, k], recvs[level].at[step, k], m_send.at[step, level, k], m_recv.at[step, level, k],
            partners[order_of(k)[level]],
        )

    def direct(step, k, j):
        return remote(
            ds.at[step - DIRECT, k, j], dr.at[step - DIRECT, k, j], d_send.at[step - DIRECT, k, j], d_recv.at[step - DIRECT, k, j],
            (tok, device_of(last_groups(k)[j])),
        )

    def hand_over_near(step):
        for q in range(4):
            @pl.when(step == 2 + q)
            def _():
                for side in range(2):
                    for a in range(2):
                        near_copy(q, a, side).wait_recv()
                        relay_copy(q, a, side).start()
                        pass_copy(q, a, side).start()

    def hand_over_far(step):
        for h in range(2):
            @pl.when(step == 6 + h)
            def _():
                for q in (2 * h, 2 * h + 1):
                    for a in range(2):
                        for side in range(2):
                            relay_copy(q, a, side).wait_recv()
                        far_copy(q, a).start()

    def arrivals(step):
        @pl.when(step == 0)
        def _():
            for h in range(2):
                for a in range(2):
                    own_copy(h, a).wait()

        @pl.when(step == 1)
        def _():
            for h in range(2):
                for a in range(2):
                    sibling_copy(h, a).wait_recv()

        for q in range(4):
            @pl.when(step == 2 + q)
            def _():
                for side in range(2):
                    for a in range(2):
                        pass_copy(q, a, side).wait_recv()

        for h in range(2):
            @pl.when(step == 6 + h)
            def _():
                for a in range(2):
                    for q in (2 * h, 2 * h + 1):
                        far_copy(q, a).wait_recv()

        @pl.when(step == 0)
        def _():
            pltpu.make_async_copy(og, g_v, load_sem.at[1]).wait()
            pltpu.make_async_copy(act, a_v, load_sem.at[0]).wait()

    def multiply(step):
        slot = step % SLOTS
        for t, (tokens, queries) in enumerate(((a_v, qi_v), (g_v, qo_v))):
            weights = queries[step].reshape(256, queries.shape[3])
            for m in range(2):
                block = lax.dot_general(
                    tokens[pl.ds(m * 512, 512), :], weights, (((1,), (1,)), ((), ())), preferred_element_type=F32
                )
                part[slot, 2 * t, pl.ds(m * 512, 512), :] = block[:, :128]
                part[slot, 2 * t + 1, pl.ds(m * 512, 512), :] = block[:, 128:]
        inverse, top_bounds = [], []
        for t in range(2):
            top = jnp.max(jnp.abs(part[slot, pl.ds(2 * t, 2)].reshape(256, 8, 128)), axis=0)
            top = jnp.max(jnp.max(top, axis=1, keepdims=True), axis=0, keepdims=True)
            bound = bound_above(jnp.broadcast_to(top, (8, 128)))
            for k in range(STREAMS):
                bounds[slot, k, t] = bound
            top_bounds.append(bound)
            inverse.append(TOP / bound)
        for k in range(STREAMS):
            s1[step, k, pl.ds(512, 16), :] = jnp.concatenate(top_bounds, axis=0).astype(BF16)
            for ct in range(4):
                for i, group in enumerate(split(k, 0)[0]):
                    value = tiles(part[slot, ct, rows_at(group, k), :])
                    s1[step, k, pl.ds(ct * 128 + i * 16, 16), :] = rows_of(encode(value, inverse[ct // 2]))
            message(step, 0, k).start()

    def total_of(step, level, k, ct, group, scale):
        n = 128 >> level
        value = tiles(part[step % SLOTS, ct, rows_at(group, k), :])
        place = pl.ds(ct * n + kept(k, level).index(group) * 16, 16)
        return value + decode(tiles(recvs[level][step, k, place, :]), scale)

    def pass_on(step, level):
        n = 128 >> level
        m = n // 2
        slot = step % SLOTS
        scales = {}
        for k in streams_at(level):
            message(step, level, k).wait()
            theirs = recvs[level][step, k, pl.ds(4 * n, 16), :].astype(F32)
            scale, inverse, fresh = [], [], []
            for t in range(2):
                their = theirs[8 * t : 8 * t + 8]
                bound = bound_above(bounds[slot, k, t] + their)
                bounds[slot, k, t] = bound
                fresh.append(bound)
                scale.append(their * (1.0 / TOP))
                inverse.append(TOP / bound)
            sends[level + 1][step, k, pl.ds(4 * m, 16), :] = jnp.concatenate(fresh, axis=0).astype(BF16)
            for ct in range(4):
                for i, group in enumerate(split(k, level + 1)[0]):
                    total = total_of(step, level, k, ct, group, scale[ct // 2])
                    sends[level + 1][step, k, pl.ds(ct * m + i * 16, 16), :] = rows_of(encode(total, inverse[ct // 2]))
            message(step, level + 1, k).start()
            scales[k] = scale
        for k in range(STREAMS):
            for ct in range(4):
                for group in split(k, level + 1)[1]:
                    total = total_of(step, level, k, ct, group, scales[k][ct // 2])
                    part[slot, ct, rows_at(group, k), :] = rows_of(total)

    def choice_of(step):
        row = lax.broadcasted_iota(jnp.int32, (256, 64), 0)
        column = lax.broadcasted_iota(jnp.int32, (256, 64), 1)
        block = row // 64
        near = jnp.logical_and(step >= 2, step < 6)
        chip = jnp.where(step < 2, x, (x + 2) % 4)
        chip = jnp.where(near, jnp.where(block < 2, flip_one(x), flip_three(x)), chip)
        side = jnp.where(near, block % 2, block // 2)
        side = jnp.where(step < 2, jnp.where(step == 0, core, 1 - core), side)
        quarter = jnp.where(near, step - 2, 2 * (step % 2) + block % 2)
        quarter = jnp.where(step < 2, block, quarter)
        query = chip * 16 + side * 8 + quarter * 2 + (row % 64) // RANK
        return jnp.where(query == column, 1.0, 0.0).astype(F32)

    def add_scores(choice):
        sums = jnp.dot(prod[...], choice, precision=lax.Precision.HIGHEST, preferred_element_type=F32)
        out[...] += sums * RANK**-0.5

    def next_bounds(step, k, theirs):
        scale, inverse, fresh = [], [], []
        for t in range(2):
            their = theirs[8 * t : 8 * t + 8]
            bound = bound_above(bounds[step % SLOTS, k, t] + their)
            fresh.append(bound)
            scale.append(their * (1.0 / TOP))
            inverse.append(TOP / bound)
        return scale, inverse, jnp.concatenate(fresh, axis=0).astype(BF16)

    def spread(step):
        level, slot = 1, step % SLOTS
        scales = {}
        for k in streams_at(level):
            message(step, level, k).wait()
            theirs = recvs[level][step, k, pl.ds(4 * 64, 16), :].astype(F32)
            scale, inverse, fresh = next_bounds(step, k, theirs)
            for j, group in enumerate(last_groups(k)):
                ds[step - DIRECT, k, j, pl.ds(64, 16), :] = fresh
                for ct in range(4):
                    total = total_of(step, level, k, ct, group, scale[ct // 2])
                    ds[step - DIRECT, k, j, pl.ds(ct * 16, 16), :] = rows_of(encode(total, inverse[ct // 2]))
                direct(step, k, j).start()
            scales[k] = scale
        for k in range(STREAMS):
            for ct in range(4):
                total = total_of(step, level, k, ct, 0, scales[k][ct // 2])
                part[slot, ct, rows_at(0, k), :] = rows_of(total)

    def finish(step):
        choice = choice_of(step)
        last = LEVELS - 1
        for k in range(STREAMS):
            message(step, last, k).wait()
            theirs = recvs[last][step, k, pl.ds(64, 16), :].astype(F32)
            scale = [theirs[:8] * (1.0 / TOP), theirs[8:] * (1.0 / TOP)]
            total = [rows_of(total_of(step, last, k, ct, 0, scale[ct // 2])) for ct in range(4)]
            for c in range(2):
                prod[pl.ds(k * 16, 16), pl.ds(c * 128, 128)] = total[c] * total[2 + c]
        add_scores(choice)

    def finish_direct(step):
        choice = choice_of(step)
        for k in range(STREAMS):
            total = [tiles(part[step % SLOTS, ct, rows_at(0, k), :]) for ct in range(4)]
            for j in range(3):
                direct(step, k, j).wait()
                theirs = dr[step - DIRECT, k, j, pl.ds(64, 16), :].astype(F32)
                scale = [theirs[:8] * (1.0 / TOP), theirs[8:] * (1.0 / TOP)]
                for ct in range(4):
                    total[ct] += decode(tiles(dr[step - DIRECT, k, j, pl.ds(ct * 16, 16), :]), scale[ct // 2])
            for c in range(2):
                prod[pl.ds(k * 16, 16), pl.ds(c * 128, 128)] = rows_of(total[c] * total[2 + c])
        add_scores(choice)

    out[...] = jnp.zeros_like(out)

    def queries_sent():
        for a in range(2):
            for h in range(2):
                sibling_copy(h, a).wait_send()
            for q in range(4):
                far_copy(q, a).wait_send()
                for side in range(2):
                    near_copy(q, a, side).wait_send()
                    pass_copy(q, a, side).wait_send()
                    relay_copy(q, a, side).wait_send()

    def of_turn(turn):
        step = turn
        fits = turn >= 0
        for idle in reversed(IDLE):
            step = jnp.where(turn > idle, step - 1, step)
            fits = jnp.logical_and(fits, turn != idle)
        return step, jnp.logical_and(fits, step < STEPS)

    def turn_body(turn, carry):
        step, fits = of_turn(turn)

        @pl.when(fits)
        def _():
            arrivals(step)
            multiply(step)

        @pl.when(turn == STEPS + len(IDLE))
        def _():
            queries_sent()

        step_n, fits_n = of_turn(turn + AHEAD)

        @pl.when(fits_n)
        def _():
            hand_over_near(step_n)

        step_0, fits_0 = of_turn(turn - LAGS[0])

        @pl.when(fits_0)
        def _():
            pass_on(step_0, 0)

        step_o, fits_o = of_turn(turn + 1)

        @pl.when(fits_o)
        def _():
            hand_over_far(step_o)

        step_1, fits_1 = of_turn(turn - LAGS[1])

        @pl.when(jnp.logical_and(fits_1, step_1 < DIRECT))
        def _():
            pass_on(step_1, 1)

        @pl.when(jnp.logical_and(fits_1, step_1 >= DIRECT))
        def _():
            spread(step_1)

        step_2, fits_2 = of_turn(turn - LAGS[2])

        @pl.when(jnp.logical_and(fits_2, step_2 < DIRECT))
        def _():
            pass_on(step_2, 2)

        step_3, fits_3 = of_turn(turn - LAGS[3])

        @pl.when(jnp.logical_and(fits_3, step_3 < DIRECT))
        def _():
            finish(step_3)

        @pl.when(jnp.logical_and(fits_2, step_2 >= DIRECT))
        def _():
            finish_direct(step_2)

        return carry

    lax.fori_loop(0, TURNS, turn_body, 0)


def shards(activations, out_grads, query_out, query_in):
    ff, d = activations.shape[1], out_grads.shape[1]
    rows = [4 * (128 >> level) + 16 for level in range(LEVELS)]
    messages = [pltpu.VMEM((STEPS, STREAMS, r, 128), BF16) for r in rows]
    return pl.pallas_call(
        kernel,
        out_shape=pltpu.VMEM((64, 64), F32),
        in_specs=[pl.BlockSpec(memory_space=pl.ANY)] * 4,
        out_specs=pl.BlockSpec(memory_space=pltpu.VMEM),
        scratch_shapes=[
            pltpu.VMEM((1024, ff), BF16),
            pltpu.VMEM((1024, d), BF16),
            pltpu.VMEM((STEPS, 4, 64, ff), BF16),
            pltpu.VMEM((STEPS, 4, 64, d), BF16),
            pltpu.VMEM((SLOTS, 4, 1024, 128), F32),
            pltpu.VMEM((SLOTS, STREAMS, 2, 8, 128), F32),
            pltpu.VMEM((64, 256), F32),
            *messages,
            *messages,
            *[pltpu.VMEM((STEPS - DIRECT, STREAMS, 3, 80, 128), BF16)] * 2,
            pltpu.SemaphoreType.DMA((2,)),
            pltpu.SemaphoreType.DMA((2, 2)),
            *[pltpu.SemaphoreType.DMA((2, 2))] * 2,
            *[pltpu.SemaphoreType.DMA((4, 2, 2))] * 6,
            *[pltpu.SemaphoreType.DMA((4, 2))] * 2,
            *[pltpu.SemaphoreType.DMA((STEPS, LEVELS, STREAMS))] * 2,
            *[pltpu.SemaphoreType.DMA((STEPS - DIRECT, STREAMS, 3))] * 2,
        ],
        compiler_params=pltpu.CompilerParams(
            collective_id=0, has_side_effects=True, vmem_limit_bytes=56 * 1024 * 1024
        ),
    )(
        activations,
        out_grads,
        query_in.reshape(4, 64, ff),
        query_out.reshape(4, 64, d),
    )


def solution(mesh):
    return jax.shard_map(
        shards,
        mesh=mesh,
        in_specs=(
            P("tok", "feat"),
            P("tok", "feat"),
            P("tok", None, "feat"),
            P("tok", None, "feat"),
        ),
        out_specs=P(("tok", "feat"), None),
        check_vma=False,
    )
```

```python
import jax
import jax.numpy as jnp
from jax import lax
from jax.experimental import pallas as pl
from jax.experimental.pallas import tpu as pltpu
from jax.sharding import PartitionSpec as P

RANK = 32
MESH = pl.DeviceIdType.MESH
F32 = jnp.float32
BF16 = jnp.bfloat16

STREAMS = 4
LEVELS = 4
STEPS = 8
LAGS = (1, 2, 3, 4)
SLOTS = 8
DIRECT = 7
POWER = 17
TOP = 2.0 ** (127.0 / POWER)
TINY = 2.0**-100
IDLE = ()
AHEAD = 1
TURNS = STEPS + len(IDLE) + LAGS[-2]


def order_of(k):
    return [(k + level) % 4 for level in range(LEVELS)]


def bit(group, d):
    return (group >> (3 - d)) % 2


def kept(k, level):
    return [g for g in range(16) if not any(bit(g, d) for d in order_of(k)[: level + 1])]


def split(k, level):
    held = range(16) if level == 0 else kept(k, level - 1)
    d = order_of(k)[level]
    return [g for g in held if bit(g, d)], [g for g in held if not bit(g, d)]


def last_groups(k):
    third, fourth = order_of(k)[2:]
    return [8 >> third, 8 >> fourth, (8 >> third) + (8 >> fourth)]


def streams_at(level):
    return sorted(range(STREAMS), key=lambda k: order_of(k)[level] % 2)


def rows_at(group, k):
    return pl.ds(group * 64 + k * 16, 16)


def flip_one(v):
    return v + 1 - 2 * (v % 2)


def flip_three(v):
    return 3 - v


def encode(value, inverse):
    n = value * inverse
    n2 = n * n
    n4 = n2 * n2
    n8 = n4 * n4
    return (n8 * n8 * n).astype(BF16)


def decode(sent, scale):
    y = sent.astype(F32)
    log = jnp.log2(jnp.maximum(jnp.abs(y), 2.0**-126))
    return y * jnp.exp2(log * (1.0 / POWER - 1.0)) * scale


def bound_above(bound):
    return jnp.maximum((bound * 1.01).astype(BF16).astype(F32), TINY)


def tiles(value):
    return value.reshape(value.shape[0] // 8, 8, 128)


def rows_of(value):
    return value.reshape(value.shape[0] * 8, 128)


def kernel(
    act, og, qi, qo, out,
    a_v, g_v, qi_v, qo_v, part, bounds, prod,
    s1, s2, s3, s4, r1, r2, r3, r4, ds, dr,
    load_sem, own_sem, sib_send, sib_recv, near_send, near_recv, pass_send, pass_recv,
    relay_send, relay_recv, far_send, far_recv, m_send, m_recv, d_send, d_recv,
):
    tok = lax.axis_index("tok")
    feat = lax.axis_index("feat")
    x, core = tok // 2, tok % 2
    z, y = feat // 4, feat % 4
    sibling = (tok + 1 - 2 * core, feat)
    near_a = (flip_one(x) * 2 + core, feat)
    near_b = (flip_three(x) * 2 + core, feat)
    partners = (
        (tok, z * 4 + flip_one(y)),
        (tok, z * 4 + flip_three(y)),
        (tok, flip_one(z) * 4 + y),
        (tok, flip_three(z) * 4 + y),
    )
    sends, recvs = (s1, s2, s3, s4), (r1, r2, r3, r4)

    def device_of(group):
        gy = flip_one(y) if bit(group, 0) else y
        gy = flip_three(gy) if bit(group, 1) else gy
        gz = flip_one(z) if bit(group, 2) else z
        gz = flip_three(gz) if bit(group, 3) else gz
        return gz * 4 + gy

    corners = tuple((tok, device_of(last_groups(k)[2])) for k in range(STREAMS))

    barrier = pltpu.get_barrier_semaphore()
    for device in (sibling, near_a, near_b) + partners + corners:
        pl.semaphore_signal(barrier, inc=1, device_id=device, device_id_type=MESH)

    arrays = ((qi, qi_v), (qo, qo_v))

    def own_copy(h, a):
        src, dst = arrays[a]
        return pltpu.make_async_copy(src.at[pl.ds(2 * h, 2)], dst.at[0, pl.ds(2 * h, 2)], own_sem.at[h, a])

    for h in range(2):
        for a in range(2):
            own_copy(h, a).start()
    for group in range(16):
        row = pl.multiple_of(device_of(group) * 64, 64)
        pltpu.make_async_copy(og.at[pl.ds(row, 64)], g_v.at[pl.ds(group * 64, 64)], load_sem.at[1]).start()
        pltpu.make_async_copy(act.at[pl.ds(row, 64)], a_v.at[pl.ds(group * 64, 64)], load_sem.at[0]).start()

    def remote(src, dst, send, recv, device):
        return pltpu.make_async_remote_copy(src, dst, send, recv, device_id=device, device_id_type=MESH)

    def sibling_copy(h, a):
        src, dst = arrays[a]
        return remote(src.at[pl.ds(2 * h, 2)], dst.at[1, pl.ds(2 * h, 2)], sib_send.at[h, a], sib_recv.at[h, a], sibling)

    def near_copy(q, a, side):
        src, dst = arrays[a]
        return remote(
            src.at[q], dst.at[2 + q, 2 * side + core], near_send.at[q, a, side], near_recv.at[q, a, side], (near_a, near_b)[side]
        )

    def pass_copy(q, a, side):
        place = arrays[a][1].at[2 + q, 2 * side + core]
        return remote(place, place, pass_send.at[q, a, side], pass_recv.at[q, a, side], sibling)

    def relay_copy(q, a, side):
        dst, half = arrays[a][1], pl.ds(32 * side, 32)
        return remote(
            dst.at[2 + q, 2 * side + core, half], dst.at[6 + q // 2, 2 * core + q % 2, half],
            relay_send.at[q, a, side], relay_recv.at[q, a, side], (near_b, near_a)[side],
        )

    def far_copy(q, a):
        place = arrays[a][1].at[6 + q // 2, 2 * core + q % 2]
        return remote(place, place, far_send.at[q, a], far_recv.at[q, a], sibling)

    pl.semaphore_wait(barrier, 11)
    for q in range(4):
        for side in range(2):
            for a in range(2):
                near_copy(q, a, side).start()
        if q < 2:
            for a in range(2):
                sibling_copy(q, a).start()

    def message(step, level, k):
        return remote(
            sends[level].at[step, k], recvs[level].at[step, k], m_send.at[step, level, k], m_recv.at[step, level, k],
            partners[order_of(k)[level]],
        )

    def direct(step, k, j):
        return remote(
            ds.at[step - DIRECT, k, j], dr.at[step - DIRECT, k, j], d_send.at[step - DIRECT, k, j], d_recv.at[step - DIRECT, k, j],
            (tok, device_of(last_groups(k)[j])),
        )

    def hand_over_near(step):
        for q in range(4):
            @pl.when(step == 2 + q)
            def _():
                for side in range(2):
                    for a in range(2):
                        near_copy(q, a, side).wait_recv()
                        relay_copy(q, a, side).start()
                        pass_copy(q, a, side).start()

    def hand_over_far(step):
        for h in range(2):
            @pl.when(step == 6 + h)
            def _():
                for q in (2 * h, 2 * h + 1):
                    for a in range(2):
                        for side in range(2):
                            relay_copy(q, a, side).wait_recv()
                        far_copy(q, a).start()

    def arrivals(step):
        @pl.when(step == 0)
        def _():
            for h in range(2):
                for a in range(2):
                    own_copy(h, a).wait()

        @pl.when(step == 1)
        def _():
            for h in range(2):
                for a in range(2):
                    sibling_copy(h, a).wait_recv()

        for q in range(4):
            @pl.when(step == 2 + q)
            def _():
                for side in range(2):
                    for a in range(2):
                        pass_copy(q, a, side).wait_recv()

        for h in range(2):
            @pl.when(step == 6 + h)
            def _():
                for a in range(2):
                    for q in (2 * h, 2 * h + 1):
                        far_copy(q, a).wait_recv()

        @pl.when(step == 0)
        def _():
            pltpu.make_async_copy(og, g_v, load_sem.at[1]).wait()
            pltpu.make_async_copy(act, a_v, load_sem.at[0]).wait()

    def multiply(step):
        slot = step % SLOTS
        for t, (tokens, queries) in enumerate(((a_v, qi_v), (g_v, qo_v))):
            weights = queries[step].reshape(256, queries.shape[3])
            for m in range(2):
                block = lax.dot_general(
                    tokens[pl.ds(m * 512, 512), :], weights, (((1,), (1,)), ((), ())), preferred_element_type=F32
                )
                part[slot, 2 * t, pl.ds(m * 512, 512), :] = block[:, :128]
                part[slot, 2 * t + 1, pl.ds(m * 512, 512), :] = block[:, 128:]
        inverse, top_bounds = [], []
        for t in range(2):
            top = jnp.max(jnp.abs(part[slot, pl.ds(2 * t, 2)].reshape(256, 8, 128)), axis=0)
            top = jnp.max(jnp.max(top, axis=1, keepdims=True), axis=0, keepdims=True)
            bound = bound_above(jnp.broadcast_to(top, (8, 128)))
            for k in range(STREAMS):
                bounds[slot, k, t] = bound
            top_bounds.append(bound)
            inverse.append(TOP / bound)
        for k in range(STREAMS):
            s1[step, k, pl.ds(512, 16), :] = jnp.concatenate(top_bounds, axis=0).astype(BF16)
            for ct in range(4):
                for i, group in enumerate(split(k, 0)[0]):
                    value = tiles(part[slot, ct, rows_at(group, k), :])
                    s1[step, k, pl.ds(ct * 128 + i * 16, 16), :] = rows_of(encode(value, inverse[ct // 2]))
            message(step, 0, k).start()

    def total_of(step, level, k, ct, group, scale):
        n = 128 >> level
        value = tiles(part[step % SLOTS, ct, rows_at(group, k), :])
        place = pl.ds(ct * n + kept(k, level).index(group) * 16, 16)
        return value + decode(tiles(recvs[level][step, k, place, :]), scale)

    def pass_on(step, level):
        n = 128 >> level
        m = n // 2
        slot = step % SLOTS
        scales = {}
        for k in streams_at(level):
            message(step, level, k).wait()
            theirs = recvs[level][step, k, pl.ds(4 * n, 16), :].astype(F32)
            scale, inverse, fresh = [], [], []
            for t in range(2):
                their = theirs[8 * t : 8 * t + 8]
                bound = bound_above(bounds[slot, k, t] + their)
                bounds[slot, k, t] = bound
                fresh.append(bound)
                scale.append(their * (1.0 / TOP))
                inverse.append(TOP / bound)
            sends[level + 1][step, k, pl.ds(4 * m, 16), :] = jnp.concatenate(fresh, axis=0).astype(BF16)
            for ct in range(4):
                for i, group in enumerate(split(k, level + 1)[0]):
                    total = total_of(step, level, k, ct, group, scale[ct // 2])
                    sends[level + 1][step, k, pl.ds(ct * m + i * 16, 16), :] = rows_of(encode(total, inverse[ct // 2]))
            message(step, level + 1, k).start()
            scales[k] = scale
        for k in range(STREAMS):
            for ct in range(4):
                for group in split(k, level + 1)[1]:
                    total = total_of(step, level, k, ct, group, scales[k][ct // 2])
                    part[slot, ct, rows_at(group, k), :] = rows_of(total)

    def choice_of(step):
        row = lax.broadcasted_iota(jnp.int32, (256, 64), 0)
        column = lax.broadcasted_iota(jnp.int32, (256, 64), 1)
        block = row // 64
        near = jnp.logical_and(step >= 2, step < 6)
        chip = jnp.where(step < 2, x, (x + 2) % 4)
        chip = jnp.where(near, jnp.where(block < 2, flip_one(x), flip_three(x)), chip)
        side = jnp.where(near, block % 2, block // 2)
        side = jnp.where(step < 2, jnp.where(step == 0, core, 1 - core), side)
        quarter = jnp.where(near, step - 2, 2 * (step % 2) + block % 2)
        quarter = jnp.where(step < 2, block, quarter)
        query = chip * 16 + side * 8 + quarter * 2 + (row % 64) // RANK
        return jnp.where(query == column, 1.0, 0.0).astype(BF16)

    def add_scores(choice):
        values = prod[...]
        high = values.astype(BF16)
        low = (values - high.astype(F32)).astype(BF16)
        sums = jnp.dot(high, choice, preferred_element_type=F32) + jnp.dot(low, choice, preferred_element_type=F32)
        out[...] += sums * RANK**-0.5

    def next_bounds(step, k, theirs):
        scale, inverse, fresh = [], [], []
        for t in range(2):
            their = theirs[8 * t : 8 * t + 8]
            bound = bound_above(bounds[step % SLOTS, k, t] + their)
            fresh.append(bound)
            scale.append(their * (1.0 / TOP))
            inverse.append(TOP / bound)
        return scale, inverse, jnp.concatenate(fresh, axis=0).astype(BF16)

    def spread(step):
        level, slot = 1, step % SLOTS
        scales = {}
        for k in streams_at(level):
            message(step, level, k).wait()
            theirs = recvs[level][step, k, pl.ds(4 * 64, 16), :].astype(F32)
            scale, inverse, fresh = next_bounds(step, k, theirs)
            for j, group in enumerate(last_groups(k)):
                ds[step - DIRECT, k, j, pl.ds(64, 16), :] = fresh
                for ct in range(4):
                    total = total_of(step, level, k, ct, group, scale[ct // 2])
                    ds[step - DIRECT, k, j, pl.ds(ct * 16, 16), :] = rows_of(encode(total, inverse[ct // 2]))
                direct(step, k, j).start()
            scales[k] = scale
        for k in range(STREAMS):
            for ct in range(4):
                total = total_of(step, level, k, ct, 0, scales[k][ct // 2])
                part[slot, ct, rows_at(0, k), :] = rows_of(total)

    def finish(step):
        choice = choice_of(step)
        last = LEVELS - 1
        for k in range(STREAMS):
            message(step, last, k).wait()
            theirs = recvs[last][step, k, pl.ds(64, 16), :].astype(F32)
            scale = [theirs[:8] * (1.0 / TOP), theirs[8:] * (1.0 / TOP)]
            total = [rows_of(total_of(step, last, k, ct, 0, scale[ct // 2])) for ct in range(4)]
            for c in range(2):
                prod[pl.ds(k * 16, 16), pl.ds(c * 128, 128)] = total[c] * total[2 + c]
        add_scores(choice)

    def finish_direct(step):
        choice = choice_of(step)
        total = {
            (k, ct): tiles(part[step % SLOTS, ct, rows_at(0, k), :]) for k in range(STREAMS) for ct in range(4)
        }
        for j in range(3):
            for k in range(STREAMS):
                direct(step, k, j).wait()
                theirs = dr[step - DIRECT, k, j, pl.ds(64, 16), :].astype(F32)
                scale = [theirs[:8] * (1.0 / TOP), theirs[8:] * (1.0 / TOP)]
                for ct in range(4):
                    total[k, ct] += decode(tiles(dr[step - DIRECT, k, j, pl.ds(ct * 16, 16), :]), scale[ct // 2])
        for k in range(STREAMS):
            for c in range(2):
                prod[pl.ds(k * 16, 16), pl.ds(c * 128, 128)] = rows_of(total[k, c] * total[k, 2 + c])
        add_scores(choice)

    out[...] = jnp.zeros_like(out)

    def queries_sent():
        for a in range(2):
            for h in range(2):
                sibling_copy(h, a).wait_send()
            for q in range(4):
                far_copy(q, a).wait_send()
                for side in range(2):
                    near_copy(q, a, side).wait_send()
                    pass_copy(q, a, side).wait_send()
                    relay_copy(q, a, side).wait_send()

    def of_turn(turn):
        step = turn
        fits = turn >= 0
        for idle in reversed(IDLE):
            step = jnp.where(turn > idle, step - 1, step)
            fits = jnp.logical_and(fits, turn != idle)
        return step, jnp.logical_and(fits, step < STEPS)

    def turn_body(turn, carry):
        step, fits = of_turn(turn)

        @pl.when(fits)
        def _():
            arrivals(step)
            multiply(step)

        @pl.when(turn == STEPS + len(IDLE))
        def _():
            queries_sent()

        step_n, fits_n = of_turn(turn + AHEAD)

        @pl.when(fits_n)
        def _():
            hand_over_near(step_n)

        step_0, fits_0 = of_turn(turn - LAGS[0])

        @pl.when(fits_0)
        def _():
            pass_on(step_0, 0)

        step_o, fits_o = of_turn(turn + 1)

        @pl.when(fits_o)
        def _():
            hand_over_far(step_o)

        step_1, fits_1 = of_turn(turn - LAGS[1])

        @pl.when(jnp.logical_and(fits_1, step_1 < DIRECT))
        def _():
            pass_on(step_1, 1)

        @pl.when(jnp.logical_and(fits_1, step_1 >= DIRECT))
        def _():
            spread(step_1)

        step_2, fits_2 = of_turn(turn - LAGS[2])

        @pl.when(jnp.logical_and(fits_2, step_2 < DIRECT))
        def _():
            pass_on(step_2, 2)

        step_3, fits_3 = of_turn(turn - LAGS[3])

        @pl.when(jnp.logical_and(fits_3, step_3 < DIRECT))
        def _():
            finish(step_3)

        @pl.when(jnp.logical_and(fits_2, step_2 >= DIRECT))
        def _():
            finish_direct(step_2)

        return carry

    lax.fori_loop(0, TURNS, turn_body, 0)


def shards(activations, out_grads, query_out, query_in):
    ff, d = activations.shape[1], out_grads.shape[1]
    rows = [4 * (128 >> level) + 16 for level in range(LEVELS)]
    messages = [pltpu.VMEM((STEPS, STREAMS, r, 128), BF16) for r in rows]
    return pl.pallas_call(
        kernel,
        out_shape=pltpu.VMEM((64, 64), F32),
        in_specs=[pl.BlockSpec(memory_space=pl.ANY)] * 4,
        out_specs=pl.BlockSpec(memory_space=pltpu.VMEM),
        scratch_shapes=[
            pltpu.VMEM((1024, ff), BF16),
            pltpu.VMEM((1024, d), BF16),
            pltpu.VMEM((STEPS, 4, 64, ff), BF16),
            pltpu.VMEM((STEPS, 4, 64, d), BF16),
            pltpu.VMEM((SLOTS, 4, 1024, 128), F32),
            pltpu.VMEM((SLOTS, STREAMS, 2, 8, 128), F32),
            pltpu.VMEM((64, 256), F32),
            *messages,
            *messages,
            *[pltpu.VMEM((STEPS - DIRECT, STREAMS, 3, 80, 128), BF16)] * 2,
            pltpu.SemaphoreType.DMA((2,)),
            pltpu.SemaphoreType.DMA((2, 2)),
            *[pltpu.SemaphoreType.DMA((2, 2))] * 2,
            *[pltpu.SemaphoreType.DMA((4, 2, 2))] * 6,
            *[pltpu.SemaphoreType.DMA((4, 2))] * 2,
            *[pltpu.SemaphoreType.DMA((STEPS, LEVELS, STREAMS))] * 2,
            *[pltpu.SemaphoreType.DMA((STEPS - DIRECT, STREAMS, 3))] * 2,
        ],
        compiler_params=pltpu.CompilerParams(
            collective_id=0, has_side_effects=True, vmem_limit_bytes=56 * 1024 * 1024
        ),
    )(
        activations,
        out_grads,
        query_in.reshape(4, 64, ff),
        query_out.reshape(4, 64, d),
    )


def solution(mesh):
    return jax.shard_map(
        shards,
        mesh=mesh,
        in_specs=(
            P("tok", "feat"),
            P("tok", "feat"),
            P("tok", None, "feat"),
            P("tok", None, "feat"),
        ),
        out_specs=P(("tok", "feat"), None),
        check_vma=False,
    )
```

```python
import jax
import jax.numpy as jnp
from jax import lax
from jax.experimental import pallas as pl
from jax.experimental.pallas import tpu as pltpu
from jax.sharding import PartitionSpec as P

RANK = 32
MESH = pl.DeviceIdType.MESH
F32 = jnp.float32
BF16 = jnp.bfloat16

STREAMS = 4
LEVELS = 4
STEPS = 8
LAGS = (1, 2, 3, 4)
SLOTS = 8
DIRECT = 7
POWER = 17
TOP = 2.0 ** (127.0 / POWER)
TINY = 2.0**-100
IDLE = ()
AHEAD = 1
TURNS = STEPS + len(IDLE) + LAGS[-2]


def order_of(k):
    return [(k + level) % 4 for level in range(LEVELS)]


def bit(group, d):
    return (group >> (3 - d)) % 2


def kept(k, level):
    return [g for g in range(16) if not any(bit(g, d) for d in order_of(k)[: level + 1])]


def split(k, level):
    held = range(16) if level == 0 else kept(k, level - 1)
    d = order_of(k)[level]
    return [g for g in held if bit(g, d)], [g for g in held if not bit(g, d)]


def last_groups(k):
    third, fourth = order_of(k)[2:]
    return [8 >> third, 8 >> fourth, (8 >> third) + (8 >> fourth)]


def streams_at(level):
    return sorted(range(STREAMS), key=lambda k: order_of(k)[level] % 2)


def rows_at(group, k):
    return pl.ds(group * 64 + k * 16, 16)


def flip_one(v):
    return v + 1 - 2 * (v % 2)


def flip_three(v):
    return 3 - v


def encode(value, inverse):
    n = value * inverse
    n2 = n * n
    n4 = n2 * n2
    n8 = n4 * n4
    return (n8 * n8 * n).astype(BF16)


def decode(sent, scale):
    y = sent.astype(F32)
    log = jnp.log2(jnp.maximum(jnp.abs(y), 2.0**-126))
    return y * jnp.exp2(log * (1.0 / POWER - 1.0)) * scale


def bound_above(bound):
    return jnp.maximum((bound * 1.01).astype(BF16).astype(F32), TINY)


def tiles(value):
    return value.reshape(value.shape[0] // 8, 8, 128)


def rows_of(value):
    return value.reshape(value.shape[0] * 8, 128)


def kernel(
    act, og, qi, qo, out,
    a_v, g_v, qi_v, qo_v, part, bounds, prod,
    s1, s2, s3, s4, r1, r2, r3, r4, ds, dr,
    load_sem, own_sem, sib_send, sib_recv, near_send, near_recv, pass_send, pass_recv,
    relay_send, relay_recv, far_send, far_recv, m_send, m_recv, d_send, d_recv,
):
    tok = lax.axis_index("tok")
    feat = lax.axis_index("feat")
    x, core = tok // 2, tok % 2
    z, y = feat // 4, feat % 4
    sibling = (tok + 1 - 2 * core, feat)
    near_a = (flip_one(x) * 2 + core, feat)
    near_b = (flip_three(x) * 2 + core, feat)
    partners = (
        (tok, z * 4 + flip_one(y)),
        (tok, z * 4 + flip_three(y)),
        (tok, flip_one(z) * 4 + y),
        (tok, flip_three(z) * 4 + y),
    )
    sends, recvs = (s1, s2, s3, s4), (r1, r2, r3, r4)

    def device_of(group):
        gy = flip_one(y) if bit(group, 0) else y
        gy = flip_three(gy) if bit(group, 1) else gy
        gz = flip_one(z) if bit(group, 2) else z
        gz = flip_three(gz) if bit(group, 3) else gz
        return gz * 4 + gy

    corners = tuple((tok, device_of(last_groups(k)[2])) for k in range(STREAMS))

    barrier = pltpu.get_barrier_semaphore()
    for device in (sibling, near_a, near_b) + partners + corners:
        pl.semaphore_signal(barrier, inc=1, device_id=device, device_id_type=MESH)

    arrays = ((qi, qi_v), (qo, qo_v))

    def own_copy(h, a):
        src, dst = arrays[a]
        return pltpu.make_async_copy(src.at[pl.ds(2 * h, 2)], dst.at[0, pl.ds(2 * h, 2)], own_sem.at[h, a])

    for h in range(2):
        for a in range(2):
            own_copy(h, a).start()
    for group in range(16):
        row = pl.multiple_of(device_of(group) * 64, 64)
        pltpu.make_async_copy(og.at[pl.ds(row, 64)], g_v.at[pl.ds(group * 64, 64)], load_sem.at[1]).start()
        pltpu.make_async_copy(act.at[pl.ds(row, 64)], a_v.at[pl.ds(group * 64, 64)], load_sem.at[0]).start()

    def remote(src, dst, send, recv, device):
        return pltpu.make_async_remote_copy(src, dst, send, recv, device_id=device, device_id_type=MESH)

    def sibling_copy(h, a):
        src, dst = arrays[a]
        return remote(src.at[pl.ds(2 * h, 2)], dst.at[1, pl.ds(2 * h, 2)], sib_send.at[h, a], sib_recv.at[h, a], sibling)

    def near_copy(q, a, side):
        src, dst = arrays[a]
        return remote(
            src.at[q], dst.at[2 + q, 2 * side + core], near_send.at[q, a, side], near_recv.at[q, a, side], (near_a, near_b)[side]
        )

    def pass_copy(q, a, side):
        place = arrays[a][1].at[2 + q, 2 * side + core]
        return remote(place, place, pass_send.at[q, a, side], pass_recv.at[q, a, side], sibling)

    def relay_copy(q, a, side):
        dst, half = arrays[a][1], pl.ds(32 * side, 32)
        return remote(
            dst.at[2 + q, 2 * side + core, half], dst.at[6 + q // 2, 2 * core + q % 2, half],
            relay_send.at[q, a, side], relay_recv.at[q, a, side], (near_b, near_a)[side],
        )

    def far_copy(q, a):
        place = arrays[a][1].at[6 + q // 2, 2 * core + q % 2]
        return remote(place, place, far_send.at[q, a], far_recv.at[q, a], sibling)

    pl.semaphore_wait(barrier, 11)
    for q in range(4):
        for side in range(2):
            for a in range(2):
                near_copy(q, a, side).start()
        if q < 2:
            for a in range(2):
                sibling_copy(q, a).start()

    def message(step, level, k):
        return remote(
            sends[level].at[step, k], recvs[level].at[step, k], m_send.at[step, level, k], m_recv.at[step, level, k],
            partners[order_of(k)[level]],
        )

    def direct(step, k, j):
        return remote(
            ds.at[step - DIRECT, k, j], dr.at[step - DIRECT, k, j], d_send.at[step - DIRECT, k, j], d_recv.at[step - DIRECT, k, j],
            (tok, device_of(last_groups(k)[j])),
        )

    def hand_over_near(step):
        for q in range(4):
            @pl.when(step == 2 + q)
            def _():
                for side in range(2):
                    for a in range(2):
                        near_copy(q, a, side).wait_recv()
                        relay_copy(q, a, side).start()
                        pass_copy(q, a, side).start()

    def hand_over_far(step):
        for h in range(2):
            @pl.when(step == 6 + h)
            def _():
                for q in (2 * h, 2 * h + 1):
                    for a in range(2):
                        for side in range(2):
                            relay_copy(q, a, side).wait_recv()
                        far_copy(q, a).start()

    def arrivals(step):
        @pl.when(step == 0)
        def _():
            for h in range(2):
                for a in range(2):
                    own_copy(h, a).wait()

        @pl.when(step == 1)
        def _():
            for h in range(2):
                for a in range(2):
                    sibling_copy(h, a).wait_recv()

        for q in range(4):
            @pl.when(step == 2 + q)
            def _():
                for side in range(2):
                    for a in range(2):
                        pass_copy(q, a, side).wait_recv()

        for h in range(2):
            @pl.when(step == 6 + h)
            def _():
                for a in range(2):
                    for q in (2 * h, 2 * h + 1):
                        far_copy(q, a).wait_recv()

        @pl.when(step == 0)
        def _():
            pltpu.make_async_copy(og, g_v, load_sem.at[1]).wait()

    def multiply(step):
        slot = step % SLOTS
        for t, tokens, queries in ((1, g_v, qo_v), (0, a_v, qi_v)):
            if t == 0:
                @pl.when(step == 0)
                def _():
                    pltpu.make_async_copy(act, a_v, load_sem.at[0]).wait()

            weights = queries[step].reshape(256, queries.shape[3])
            for m in range(2):
                block = lax.dot_general(
                    tokens[pl.ds(m * 512, 512), :], weights, (((1,), (1,)), ((), ())), preferred_element_type=F32
                )
                part[slot, 2 * t, pl.ds(m * 512, 512), :] = block[:, :128]
                part[slot, 2 * t + 1, pl.ds(m * 512, 512), :] = block[:, 128:]
        inverse, top_bounds = [], []
        for t in range(2):
            top = jnp.max(jnp.abs(part[slot, pl.ds(2 * t, 2)].reshape(256, 8, 128)), axis=0)
            top = jnp.max(jnp.max(top, axis=1, keepdims=True), axis=0, keepdims=True)
            bound = bound_above(jnp.broadcast_to(top, (8, 128)))
            for k in range(STREAMS):
                bounds[slot, k, t] = bound
            top_bounds.append(bound)
            inverse.append(TOP / bound)
        for k in range(STREAMS):
            s1[step, k, pl.ds(512, 16), :] = jnp.concatenate(top_bounds, axis=0).astype(BF16)
            for ct in range(4):
                for i, group in enumerate(split(k, 0)[0]):
                    value = tiles(part[slot, ct, rows_at(group, k), :])
                    s1[step, k, pl.ds(ct * 128 + i * 16, 16), :] = rows_of(encode(value, inverse[ct // 2]))
            message(step, 0, k).start()

    def total_of(step, level, k, ct, group, scale):
        n = 128 >> level
        value = tiles(part[step % SLOTS, ct, rows_at(group, k), :])
        place = pl.ds(ct * n + kept(k, level).index(group) * 16, 16)
        return value + decode(tiles(recvs[level][step, k, place, :]), scale)

    def pass_on(step, level):
        n = 128 >> level
        m = n // 2
        slot = step % SLOTS
        scales = {}
        for k in streams_at(level):
            message(step, level, k).wait()
            theirs = recvs[level][step, k, pl.ds(4 * n, 16), :].astype(F32)
            scale, inverse, fresh = [], [], []
            for t in range(2):
                their = theirs[8 * t : 8 * t + 8]
                bound = bound_above(bounds[slot, k, t] + their)
                bounds[slot, k, t] = bound
                fresh.append(bound)
                scale.append(their * (1.0 / TOP))
                inverse.append(TOP / bound)
            sends[level + 1][step, k, pl.ds(4 * m, 16), :] = jnp.concatenate(fresh, axis=0).astype(BF16)
            for ct in range(4):
                for i, group in enumerate(split(k, level + 1)[0]):
                    total = total_of(step, level, k, ct, group, scale[ct // 2])
                    sends[level + 1][step, k, pl.ds(ct * m + i * 16, 16), :] = rows_of(encode(total, inverse[ct // 2]))
            message(step, level + 1, k).start()
            scales[k] = scale
        for k in range(STREAMS):
            for ct in range(4):
                for group in split(k, level + 1)[1]:
                    total = total_of(step, level, k, ct, group, scales[k][ct // 2])
                    part[slot, ct, rows_at(group, k), :] = rows_of(total)

    def choice_of(step):
        row = lax.broadcasted_iota(jnp.int32, (256, 64), 0)
        column = lax.broadcasted_iota(jnp.int32, (256, 64), 1)
        block = row // 64
        near = jnp.logical_and(step >= 2, step < 6)
        chip = jnp.where(step < 2, x, (x + 2) % 4)
        chip = jnp.where(near, jnp.where(block < 2, flip_one(x), flip_three(x)), chip)
        side = jnp.where(near, block % 2, block // 2)
        side = jnp.where(step < 2, jnp.where(step == 0, core, 1 - core), side)
        quarter = jnp.where(near, step - 2, 2 * (step % 2) + block % 2)
        quarter = jnp.where(step < 2, block, quarter)
        query = chip * 16 + side * 8 + quarter * 2 + (row % 64) // RANK
        return jnp.where(query == column, 1.0, 0.0).astype(BF16)

    def add_scores(choice):
        values = prod[...]
        high = values.astype(BF16)
        low = (values - high.astype(F32)).astype(BF16)
        sums = jnp.dot(high, choice, preferred_element_type=F32) + jnp.dot(low, choice, preferred_element_type=F32)
        out[...] += sums * RANK**-0.5

    def next_bounds(step, k, theirs):
        scale, inverse, fresh = [], [], []
        for t in range(2):
            their = theirs[8 * t : 8 * t + 8]
            bound = bound_above(bounds[step % SLOTS, k, t] + their)
            fresh.append(bound)
            scale.append(their * (1.0 / TOP))
            inverse.append(TOP / bound)
        return scale, inverse, jnp.concatenate(fresh, axis=0).astype(BF16)

    def spread(step):
        level, slot = 1, step % SLOTS
        scales = {}
        for k in streams_at(level):
            message(step, level, k).wait()
            theirs = recvs[level][step, k, pl.ds(4 * 64, 16), :].astype(F32)
            scale, inverse, fresh = next_bounds(step, k, theirs)
            for j, group in enumerate(last_groups(k)):
                ds[step - DIRECT, k, j, pl.ds(64, 16), :] = fresh
                for ct in range(4):
                    total = total_of(step, level, k, ct, group, scale[ct // 2])
                    ds[step - DIRECT, k, j, pl.ds(ct * 16, 16), :] = rows_of(encode(total, inverse[ct // 2]))
                direct(step, k, j).start()
            scales[k] = scale
        for k in range(STREAMS):
            for ct in range(4):
                total = total_of(step, level, k, ct, 0, scales[k][ct // 2])
                part[slot, ct, rows_at(0, k), :] = rows_of(total)

    def finish(step):
        choice = choice_of(step)
        last = LEVELS - 1
        for k in range(STREAMS):
            message(step, last, k).wait()
            theirs = recvs[last][step, k, pl.ds(64, 16), :].astype(F32)
            scale = [theirs[:8] * (1.0 / TOP), theirs[8:] * (1.0 / TOP)]
            total = [rows_of(total_of(step, last, k, ct, 0, scale[ct // 2])) for ct in range(4)]
            for c in range(2):
                prod[pl.ds(k * 16, 16), pl.ds(c * 128, 128)] = total[c] * total[2 + c]
        add_scores(choice)

    def finish_direct(step):
        choice = choice_of(step)
        total = {
            (k, ct): tiles(part[step % SLOTS, ct, rows_at(0, k), :]) for k in range(STREAMS) for ct in range(4)
        }
        for j in range(3):
            for k in range(STREAMS):
                direct(step, k, j).wait()
                theirs = dr[step - DIRECT, k, j, pl.ds(64, 16), :].astype(F32)
                scale = [theirs[:8] * (1.0 / TOP), theirs[8:] * (1.0 / TOP)]
                for ct in range(4):
                    total[k, ct] += decode(tiles(dr[step - DIRECT, k, j, pl.ds(ct * 16, 16), :]), scale[ct // 2])
        for k in range(STREAMS):
            for c in range(2):
                prod[pl.ds(k * 16, 16), pl.ds(c * 128, 128)] = rows_of(total[k, c] * total[k, 2 + c])
        add_scores(choice)

    out[...] = jnp.zeros_like(out)

    def queries_sent():
        for a in range(2):
            for h in range(2):
                sibling_copy(h, a).wait_send()
            for q in range(4):
                far_copy(q, a).wait_send()
                for side in range(2):
                    near_copy(q, a, side).wait_send()
                    pass_copy(q, a, side).wait_send()
                    relay_copy(q, a, side).wait_send()

    def of_turn(turn):
        step = turn
        fits = turn >= 0
        for idle in reversed(IDLE):
            step = jnp.where(turn > idle, step - 1, step)
            fits = jnp.logical_and(fits, turn != idle)
        return step, jnp.logical_and(fits, step < STEPS)

    def turn_body(turn, carry):
        step, fits = of_turn(turn)

        @pl.when(fits)
        def _():
            arrivals(step)
            multiply(step)

        @pl.when(turn == STEPS + len(IDLE))
        def _():
            queries_sent()

        step_n, fits_n = of_turn(turn + AHEAD)

        @pl.when(fits_n)
        def _():
            hand_over_near(step_n)

        step_0, fits_0 = of_turn(turn - LAGS[0])

        @pl.when(fits_0)
        def _():
            pass_on(step_0, 0)

        step_o, fits_o = of_turn(turn + 1)

        @pl.when(fits_o)
        def _():
            hand_over_far(step_o)

        step_1, fits_1 = of_turn(turn - LAGS[1])

        @pl.when(jnp.logical_and(fits_1, step_1 < DIRECT))
        def _():
            pass_on(step_1, 1)

        @pl.when(jnp.logical_and(fits_1, step_1 >= DIRECT))
        def _():
            spread(step_1)

        step_2, fits_2 = of_turn(turn - LAGS[2])

        @pl.when(jnp.logical_and(fits_2, step_2 < DIRECT))
        def _():
            pass_on(step_2, 2)

        step_3, fits_3 = of_turn(turn - LAGS[3])

        @pl.when(jnp.logical_and(fits_3, step_3 < DIRECT))
        def _():
            finish(step_3)

        @pl.when(jnp.logical_and(fits_2, step_2 >= DIRECT))
        def _():
            finish_direct(step_2)

        return carry

    lax.fori_loop(0, TURNS, turn_body, 0)


def shards(activations, out_grads, query_out, query_in):
    ff, d = activations.shape[1], out_grads.shape[1]
    rows = [4 * (128 >> level) + 16 for level in range(LEVELS)]
    messages = [pltpu.VMEM((STEPS, STREAMS, r, 128), BF16) for r in rows]
    return pl.pallas_call(
        kernel,
        out_shape=pltpu.VMEM((64, 64), F32),
        in_specs=[pl.BlockSpec(memory_space=pl.ANY)] * 4,
        out_specs=pl.BlockSpec(memory_space=pltpu.VMEM),
        scratch_shapes=[
            pltpu.VMEM((1024, ff), BF16),
            pltpu.VMEM((1024, d), BF16),
            pltpu.VMEM((STEPS, 4, 64, ff), BF16),
            pltpu.VMEM((STEPS, 4, 64, d), BF16),
            pltpu.VMEM((SLOTS, 4, 1024, 128), F32),
            pltpu.VMEM((SLOTS, STREAMS, 2, 8, 128), F32),
            pltpu.VMEM((64, 256), F32),
            *messages,
            *messages,
            *[pltpu.VMEM((STEPS - DIRECT, STREAMS, 3, 80, 128), BF16)] * 2,
            pltpu.SemaphoreType.DMA((2,)),
            pltpu.SemaphoreType.DMA((2, 2)),
            *[pltpu.SemaphoreType.DMA((2, 2))] * 2,
            *[pltpu.SemaphoreType.DMA((4, 2, 2))] * 6,
            *[pltpu.SemaphoreType.DMA((4, 2))] * 2,
            *[pltpu.SemaphoreType.DMA((STEPS, LEVELS, STREAMS))] * 2,
            *[pltpu.SemaphoreType.DMA((STEPS - DIRECT, STREAMS, 3))] * 2,
        ],
        compiler_params=pltpu.CompilerParams(
            collective_id=0, has_side_effects=True, vmem_limit_bytes=56 * 1024 * 1024
        ),
    )(
        activations,
        out_grads,
        query_in.reshape(4, 64, ff),
        query_out.reshape(4, 64, d),
    )


def solution(mesh):
    return jax.shard_map(
        shards,
        mesh=mesh,
        in_specs=(
            P("tok", "feat"),
            P("tok", "feat"),
            P("tok", None, "feat"),
            P("tok", None, "feat"),
        ),
        out_specs=P(("tok", "feat"), None),
        check_vma=False,
    )
```
